128 devices in a mesh: flow: 16 (over z, y), group: 8 (over x, core).
Axes of the slice: x: 4, y: 4, z: 4, core: 2. Of those that a mesh axis runs over, the one named last changes fastest.
Arguments:
- cell_state: float32 [12, 524288], P(None, 'flow'), may hold values from 0.1 to 10
- inflow: float32 [12, 8192], P(None, ('flow', 'group')), may hold values from 0.1 to 10
- courant: float32 [256, 8192], P(None, ('flow', 'group')), may hold values from 1 to 15360
- pick: int32 [8, 16, 16, 1024], P('group', 'flow'), may hold values from 0 to 32767, as said below
- node_slot: int32 [256, 8192], P(None, ('flow', 'group')), may hold values from 0 to 16383, as said below
- stoich: float32 [6, 12], replicated, may hold values from 0 to 0.25
- logk: float32 [6], replicated, may hold values from -3 to 0
Outputs:
- cell_species: float32 [18, 524288], P(None, ('flow', 'group'))
The draws below stay inside these ranges and needn't reach their ends.
Inputs may be any that keep to these rules, and one draw needn't show every extreme that they name: pick[g, a, b, k] lies in the block of 128 local cells numbered ((b * 1024 + k) // 128 + g * 128) modulo (256). With j = s % 64, node_slot[n, s] lies in the tile of 128 records numbered (n * 64 + j) // 128.
All inputs are finite; a program needn't handle non-finite values.
Results may differ from the reference program's by a relative error of at most 0.00011.
Values sent between devices are 32-bit elements; how exact they have to be, the bound alone decides.
No kernel may reach another device: no remote copies, remote signals or barrier semaphores. Data moves between devices by JAX's collectives and lax.ppermute only.
A program may use at most 128 MiB of HBM per device.

```python
import math
import jax
import jax.numpy as jnp
from jax import lax

NC = 12
NX = 6
NODES = 256
ITERS = 4
WIN = 128
SL_DEV = 64
CELL_DEV = 32768
SLOTS = 16384
CAP = 1024
SL = 8192
CELLS = 524288
N_FLOW = 16
N_GROUP = 8


def draw_courant(key, part):
    key = jax.random.fold_in(key, 7)
    first, second = jax.random.split(key)
    lowest = math.log(2.0)
    speed = jnp.exp(jax.random.uniform(first, (1, SL), jnp.float32, lowest, math.log(30.0 * NODES)))
    rough = jax.random.uniform(second, (NODES, SL), jnp.float32, 0.5, 2.0)
    return (speed * rough).astype(jnp.float32)


def draw_pick(key, part):
    key = jax.random.fold_in(key, 11)
    shape = (N_GROUP, N_FLOW, N_FLOW, CAP)
    group_ids = jax.lax.broadcasted_iota(jnp.int32, shape, 0)
    target = jax.lax.broadcasted_iota(jnp.int32, shape, 2)
    record = jax.lax.broadcasted_iota(jnp.int32, shape, 3)
    tiles = (target * CAP + record) // WIN
    blocks = (tiles + group_ids * (SLOTS // WIN)) % (CELL_DEV // WIN)
    inside = jax.random.randint(key, shape, 0, WIN, dtype=jnp.int32)
    return (blocks * WIN + inside).astype(jnp.int32)


def draw_node_slot(key, part):
    key = jax.random.fold_in(key, 13)
    shape = (NODES, SL)
    node_ids = jax.lax.broadcasted_iota(jnp.int32, shape, 0)
    line_ids = jax.lax.broadcasted_iota(jnp.int32, shape, 1)
    tiles = (node_ids * SL_DEV + line_ids % SL_DEV) // WIN
    inside = jax.random.randint(key, shape, 0, WIN, dtype=jnp.int32)
    return (tiles * WIN + inside).astype(jnp.int32)


def shard_levels(stream_key, extent, cuts, least, high):
    def one(axis_at, shards_of):
        draws = jax.random.uniform(jax.random.fold_in(jax.random.fold_in(stream_key, 6), axis_at), (shards_of,), jnp.float32, least / len(cuts), high / len(cuts))
        return jnp.repeat(jnp.exp(draws), extent[axis_at] // shards_of).reshape((-1,) + (1,) * (len(extent) - axis_at - 1))

    loudness = one(*cuts[0])
    for cut in cuts[1:]:
        loudness = loudness * one(*cut)
    return loudness


def setup_inputs(seed: int = 0) -> dict:
    key_of = jax.random.split(jax.random.key(seed), 8)
    cell_state = jnp.clip(jnp.exp(math.log(10.0) - 4.6051702 * jax.random.uniform(key_of[0], (NC, CELLS), jnp.float32) ** shard_levels(key_of[0], (NC, CELLS), ((1, 16),), -0.2, 0.2)), 0.1, 10.0)
    inflow = jnp.clip(jnp.exp(math.log(10.0) - 4.6051702 * jax.random.uniform(key_of[1], (NC, SL), jnp.float32) ** shard_levels(key_of[1], (NC, SL), ((1, 128),), -0.2, 0.2)), 0.1, 10.0)
    courant = draw_courant(jax.random.fold_in(key_of[7], 71), 0)
    pick = draw_pick(jax.random.fold_in(key_of[7], 71), 0)
    node_slot = draw_node_slot(jax.random.fold_in(key_of[7], 71), 0)
    stoich = jnp.clip(jax.random.uniform(key_of[5], (NX, NC), jnp.float32, 0.0, 0.25), 0.0, 0.25)
    logk = jnp.clip(jax.random.uniform(key_of[6], (NX,), jnp.float32, -3.0, 0.0), -3.0, 0.0)
    return dict(cell_state=cell_state, inflow=inflow, courant=courant, pick=pick, node_slot=node_slot, stoich=stoich, logk=logk)


def solve_spd(matrix, rhs):
    order = len(rhs)
    lower = {}
    inverse = []
    for outer in range(order):
        for inner in range(outer + 1):
            total = matrix[outer, inner]
            for other in range(inner):
                total = total - lower[outer, other] * lower[inner, other]
            if outer == inner:
                inverse.append(lax.rsqrt(total))
            else:
                lower[outer, inner] = total * inverse[inner]
    middle = []
    for outer in range(order):
        total = rhs[outer]
        for other in range(outer):
            total = total - lower[outer, other] * middle[other]
        middle.append(total * inverse[outer])
    result = [None] * order
    for outer in reversed(range(order)):
        total = middle[outer]
        for other in range(outer + 1, order):
            total = total - lower[other, outer] * result[other]
        result[outer] = total * inverse[outer]
    return result

def speciate(totals, stoich, logk):
    count_comp = totals.shape[0]
    identity = jnp.eye(count_comp, dtype=jnp.float32)
    logfree = jnp.log(totals)
    for sweep in range(ITERS):
        free = jnp.exp(logfree)
        complexes = jnp.exp(logk[:, None] + jnp.dot(stoich, logfree, precision=lax.Precision.HIGHEST, preferred_element_type=jnp.float32))
        mismatch = free + jnp.dot(stoich.T, complexes, precision=lax.Precision.HIGHEST, preferred_element_type=jnp.float32) - totals
        jacobian = jnp.einsum('pi,pj,pn->ijn', stoich, stoich, complexes, precision=lax.Precision.HIGHEST)
        jacobian = jacobian + identity[:, :, None] * free[:, None, :]
        update = solve_spd(jacobian, [-mismatch[comp] for comp in range(count_comp)])
        logfree = logfree + jnp.stack(update)
    complexes = jnp.exp(logk[:, None] + jnp.dot(stoich, logfree, precision=lax.Precision.HIGHEST, preferred_element_type=jnp.float32))
    return jnp.concatenate([jnp.exp(logfree), complexes], axis=0)

def reference(cell_state, inflow, courant, pick, node_slot, stoich, logk):
    count_comp = cell_state.shape[0]
    line_ids = lax.broadcasted_iota(jnp.int32, (NODES, SL), 1)
    device_id = (line_ids // SL_DEV).astype(jnp.int32)
    flow_id = (device_id // N_GROUP).astype(jnp.int32)
    group_id = (device_id % N_GROUP).astype(jnp.int32)
    anchor = (node_slot // CAP).astype(jnp.int32)
    record = (node_slot % CAP).astype(jnp.int32)
    cell = (anchor * CELL_DEV + pick[group_id, anchor, flow_id, record]).astype(jnp.int32)
    old = cell_state[:, cell]
    weight = courant / (1.0 + courant)
    source = old / (1.0 + courant)[None]

    def advance(carry, inputs):
        node_weight, node_source = inputs
        moved = node_weight[None] * carry + node_source
        return (moved, moved)
    last, moved = lax.scan(advance, inflow, (weight, jnp.transpose(source, (1, 0, 2))))
    moved = jnp.transpose(moved, (1, 0, 2))
    devices = SL // SL_DEV
    blocks = moved.reshape(count_comp, NODES, devices, SL_DEV)
    blocks = jnp.transpose(blocks, (2, 0, 1, 3)).reshape(devices, count_comp, NODES * SL_DEV)
    species = lax.map(lambda block: speciate(block, stoich, logk), blocks)
    width = species.shape[1]
    species = species.reshape(devices, width, NODES, SL_DEV)
    species = jnp.transpose(species, (1, 2, 0, 3)).reshape(width, NODES * SL)
    flat_cell = cell.reshape(-1)
    totals = jnp.zeros((width, CELLS), jnp.float32).at[:, flat_cell].add(species)
    counts = jnp.zeros((CELLS,), jnp.float32).at[flat_cell].add(jnp.ones((NODES * SL,), jnp.float32))
    return totals / jnp.maximum(counts, 1.0)[None]
```

```python
import functools

import jax
import jax.numpy as jnp
from jax import lax
from jax.experimental import pallas as pl
from jax.experimental.pallas import tpu as pltpu
from jax.sharding import Mesh, PartitionSpec as P

ITERS = 4
WIN = 128
NC = 12
NX = 6
NQ = NC + NX + 1
PAD = 24
SIDE = 4
FLOW = 16
SUB = 8
HALF = 64
BATCH = 8
BF16 = jnp.bfloat16
F32 = jnp.float32


def split(value, parts):
    out = []
    for part in range(parts):
        out.append(value.astype(BF16))
        if part < parts - 1:
            value = value - out[-1].astype(F32)
    return out


def dot(left, right):
    return jnp.dot(left, right, preferred_element_type=F32)


ALL = [(0, 0), (0, 1), (0, 2), (1, 0), (1, 1), (2, 0)]
MOST = ALL[:5]


def stack(parts, terms):
    return jnp.concatenate([parts[right] for _, right in terms], axis=0)


def tables(stoich):
    eye = jnp.eye(SUB, dtype=F32)

    def table(small, terms):
        rows, columns = small.shape
        value = small[:, None, :, None] * eye[None, :, None, :]
        value = value.reshape(rows * SUB, columns * SUB)
        parts = []
        for _ in range(3):
            part = lax.reduce_precision(value, 8, 7)
            parts.append(part.astype(BF16))
            value = value - part
        return jnp.concatenate([parts[left] for left, _ in terms], axis=1)

    gram = jnp.stack([stoich[p] * stoich[q] for p, q in pairs(NX)])
    cross = jnp.stack([stoich[:, i] * stoich[:, j] for i, j in pairs(NC)])
    return table(gram, ALL), table(cross, MOST), table(stoich.T, ALL)


def pairs(order):
    return [(i, j) for i in range(order) for j in range(i + 1)]


def solve_spd(matrix, rhs):
    order = len(rhs)
    lower, inverse, middle = {}, [], []
    for outer in range(order):
        scaled = {}
        for inner in range(outer):
            total = matrix(outer, inner)
            for other in range(inner):
                total = total - scaled[other] * lower[inner, other]
            scaled[inner] = total
            lower[outer, inner] = total * inverse[inner]
        total = matrix(outer, outer)
        value = rhs[outer]
        for other in range(outer):
            total = total - scaled[other] * lower[outer, other]
            value = value - lower[outer, other] * middle[other]
        inverse.append(1.0 / total)
        middle.append(value)
    result = [None] * order
    for outer in reversed(range(order)):
        total = middle[outer] * inverse[outer]
        for other in range(outer + 1, order):
            total = total - lower[other, outer] * result[other]
        result[outer] = total
    return result


def entries(value, diagonal):
    order = len(diagonal)
    at = {pair: SUB * k for k, pair in enumerate(pairs(order))}

    def entry(i, j):
        part = value[at[i, j] : at[i, j] + SUB]
        return part + diagonal[i] if i == j else part

    return entry


def speciate(totals, stoich, logk, gram, cross, back):
    def log_complexes(logfree):
        out = []
        for p in range(NX):
            total = logk(p)
            for i in range(NC):
                total = total + stoich(p, i) * logfree[i]
            out.append(total)
        return out

    def spread(parts):
        taken = dot(back, stack(parts, ALL))
        return [taken[SUB * i : SUB * (i + 1)] for i in range(NC)]

    logfree = [jnp.log(t) for t in totals]
    invfree = [1.0 / t for t in totals]
    weights = dot(gram, stack(split(jnp.concatenate(invfree, axis=0), 3), ALL))
    inverse = [jnp.exp(-jnp.maximum(v, -80.0)) for v in log_complexes(logfree)]
    bound = solve_spd(entries(weights, inverse), [jnp.ones_like(totals[0])] * NX)
    taken = spread(split(jnp.concatenate(bound, axis=0), 3))
    logfree = [x - b * v for x, b, v in zip(logfree, taken, invfree)]
    for sweep in range(ITERS - 1):
        free = [jnp.exp(x) for x in logfree]
        complexes = [jnp.exp(v) for v in log_complexes(logfree)]
        parts = split(jnp.concatenate(complexes, axis=0), 3)
        jacobian = entries(dot(cross, stack(parts, MOST)), free)
        excess = [(t - f) - b for t, f, b in zip(totals, free, spread(parts))]
        logfree = [x + d for x, d in zip(logfree, solve_spd(jacobian, excess))]
    return [jnp.exp(x) for x in logfree] + [jnp.exp(v) for v in log_complexes(logfree)]


def react_kernel(
    recv_ref, lanes_ref, message_ref, gram_ref, cross_ref, back_ref, stoich_ref, logk_ref,
    out_ref, coef, carry, rows_buf,
):
    lane = lax.broadcasted_iota(jnp.int32, (SUB, WIN), 1)
    row = lax.broadcasted_iota(jnp.int32, (SUB, WIN), 0)
    cell = lax.broadcasted_iota(jnp.int32, (WIN, WIN), 0)
    odd = lane >= HALF
    for p in range(NX):
        for i in range(NC):
            coef[p * NC + i] = jnp.full((SUB, WIN), stoich_ref[p, i], F32)
        coef[NX * NC + p] = jnp.full((SUB, WIN), logk_ref[p], F32)
    for c in range(NC):
        carry[c] = jnp.broadcast_to(message_ref[pl.ds(256 + c, 1), :], (SUB, WIN))
    rows_buf[...] = jnp.zeros(rows_buf.shape, F32)
    for b in range(BATCH):
        rows_buf[pl.ds(b * SUB * PAD + NQ - 1, SUB, stride=PAD), :] = jnp.ones((SUB, WIN), F32)

    def swap(value):
        return pltpu.roll(value, HALF, 1)

    def wide(value):
        return jnp.concatenate([value] * BATCH, axis=1)

    def step(index, unused):
        moved = [[] for _ in range(NC)]
        places = []
        for b in range(BATCH):
            source = index * BATCH + b
            base = pl.multiple_of(source * SUB, SUB)
            slot = message_ref[pl.ds(base, SUB), :].astype(jnp.int32)
            local = jnp.take_along_axis(lanes_ref[source], slot, axis=1).astype(jnp.int32)
            places.append(local)
            courant = message_ref[pl.ds(base + WIN, SUB), :]
            ratio = 1.0 / (1.0 + courant)
            weight = courant * ratio
            pair = jnp.where(odd, weight * swap(weight), weight)
            run = jnp.where(odd, pair, swap(pair))
            factors = []
            for reach in (1, 2, 4):
                factors.append(jnp.where(row >= reach, run, 0.0))
                run = run * jnp.where(row >= reach, pltpu.roll(run, reach, 0), 1.0)
            for c in range(NC):
                part = jnp.take_along_axis(recv_ref[source, c], local, axis=1) * ratio
                part = jnp.where(odd, weight * swap(part) + part, part)
                total = jnp.where(odd, part, swap(part))
                for level, reach in enumerate((1, 2, 4)):
                    total = total + factors[level] * pltpu.roll(total, reach, 0)
                before = carry[c]
                total = total + run * before
                carry[c] = jnp.broadcast_to(total[SUB - 1 :, :], (SUB, WIN))
                ahead = jnp.where(row == 0, before, pltpu.roll(total, 1, 0))
                moved[c].append(part + pair * ahead)
        species = speciate(
            [jnp.concatenate(parts, axis=1) for parts in moved],
            lambda p, i: wide(coef[p * NC + i]),
            lambda p: wide(coef[NX * NC + p]),
            gram_ref[...],
            cross_ref[...],
            back_ref[...],
        )
        for q in range(NC + NX):
            for b in range(BATCH):
                rows_buf[pl.ds(b * SUB * PAD + q, SUB, stride=PAD), :] = species[q][
                    :, b * WIN : (b + 1) * WIN
                ]
        for b in range(BATCH):
            for kt in range(SUB):
                hot = (cell == jnp.broadcast_to(places[b][kt : kt + 1, :], (WIN, WIN))).astype(BF16)
                value = rows_buf[pl.ds((b * SUB + kt) * PAD, PAD), :]
                both = lax.dot_general(
                    jnp.concatenate(split(value, 2), axis=0),
                    hot,
                    (((1,), (1,)), ((), ())),
                    preferred_element_type=F32,
                )
                sums = both[:PAD] + both[PAD:]
                out_ref[index * BATCH + b, pl.ds(kt, NQ, stride=SUB), :] = sums[:NQ]
        return unused

    lax.fori_loop(0, FLOW // BATCH, step, 0)


def react(recv, lanes, message, stoich, logk):
    return pl.pallas_call(
        react_kernel,
        out_shape=jax.ShapeDtypeStruct((FLOW, NQ * SUB, WIN), F32),
        in_specs=[pl.BlockSpec(memory_space=pltpu.VMEM)] * 6
        + [pl.BlockSpec(memory_space=pltpu.SMEM)] * 2,
        scratch_shapes=[
            pltpu.VMEM((NX * NC + NX, SUB, WIN), F32),
            pltpu.VMEM((NC, SUB, WIN), F32),
            pltpu.VMEM((BATCH * SUB * PAD, WIN), F32),
        ],
        compiler_params=pltpu.CompilerParams(vmem_limit_bytes=32 * 1024 * 1024),
        name="react",
    )(recv, lanes, message, *tables(stoich), stoich, logk)


def body(cell_state, inflow, courant, pick, node_slot, stoich, logk):
    block = SIDE * SUB * WIN
    column = lax.axis_index("h") * SIDE + lax.axis_index("q")
    mine = lax.dynamic_slice_in_dim(cell_state, column * block, block, 1)
    mine = jnp.transpose(mine.reshape(NC, SIDE, SUB, WIN), (1, 0, 2, 3))
    send = jnp.broadcast_to(mine[None], (SIDE, SIDE, NC, SUB, WIN)).reshape(FLOW, NC, SUB, WIN)
    recv = lax.all_to_all(send, ("z", "y"), 0, 0, tiled=True)
    start = jnp.concatenate([inflow, inflow], axis=1)
    start = jnp.concatenate([start, start[:4]], axis=0)
    low = WIN - 1
    message = jnp.concatenate(
        [
            jnp.bitwise_and(node_slot, low).astype(F32).reshape(WIN, WIN),
            courant.reshape(WIN, WIN),
            start,
            jnp.bitwise_and(pick, low).astype(F32).reshape(WIN, WIN),
        ],
        axis=0,
    )
    route = []
    for z in range(SIDE):
        for y in range(SIDE):
            for x in range(SIDE):
                for h in range(2):
                    source = (z * SIDE + y) * 2 * SIDE + x * 2 + h
                    route.append((source, (x * SIDE + y) * 2 * SIDE + h * SIDE + z))
    message = lax.ppermute(message, ("z", "y", "h", "q"), route)
    recv, message = lax.optimization_barrier((recv, message))
    lanes = message[2 * WIN + FLOW :].reshape(FLOW, SUB, WIN)
    lanes = lax.all_to_all(lanes, ("q", "y"), 0, 0, tiled=True)
    sums = react(recv, lanes, message[: 2 * WIN + FLOW], stoich, logk)
    back = lax.all_to_all(sums, ("z", "y"), 0, 0, tiled=True)
    back = jnp.sum(back.reshape(SIDE, SIDE, NQ, SUB * WIN), axis=0)
    means = back[:, : NQ - 1] / jnp.maximum(back[:, NQ - 1 :], 1.0)
    return jnp.transpose(means, (1, 0, 2)).reshape(NQ - 1, block)


def solution(mesh):
    grid = Mesh(mesh.devices.reshape(SIDE, SIDE, 2, SIDE), ("z", "y", "h", "q"))
    flow, group = ("z", "y"), ("h", "q")
    every = P(None, flow + group)
    placed = (P(None, flow), every, every, P(group, flow, None, None), every, P(), P())
    return jax.shard_map(body, mesh=grid, in_specs=placed, out_specs=every, check_vma=False)
```

```python
import functools

import jax
import jax.numpy as jnp
from jax import lax
from jax.experimental import pallas as pl
from jax.experimental.pallas import tpu as pltpu
from jax.sharding import Mesh, PartitionSpec as P

ITERS = 4
WIN = 128
NC = 12
NX = 6
NQ = NC + NX + 1
PAD = 24
SIDE = 4
FLOW = 16
SUB = 8
HALF = 64
LANES = 2 * WIN + FLOW
BATCH = 8
BF16 = jnp.bfloat16
F32 = jnp.float32


def split(value, parts):
    out = []
    for part in range(parts):
        out.append(value.astype(BF16))
        if part < parts - 1:
            value = value - out[-1].astype(F32)
    return out


def dot(left, right):
    return jnp.dot(left, right, preferred_element_type=F32)


ALL = [(0, 0), (0, 1), (0, 2), (1, 0), (1, 1), (2, 0)]
MOST = ALL[:5]


def stack(parts, terms):
    return jnp.concatenate([parts[right] for _, right in terms], axis=0)


def build_tables(stoich_ref, gram_ref, cross_ref, back_ref):
    def spread(count, terms, pick):
        lane = lax.broadcasted_iota(jnp.int32, (SUB, len(terms) * count * SUB), 1)
        row = lax.broadcasted_iota(jnp.int32, lane.shape, 0)
        which = lane % (count * SUB) // SUB
        vectors = []
        for outer in range(NC + NX - count):
            value = jnp.zeros(lane.shape, F32)
            for inner in range(count):
                value = jnp.where(which == inner, pick(outer, inner), value)
            vectors.append(value)
        return vectors, lane // (count * SUB), lane % SUB == row

    def write(ref, values, term, same, terms):
        for at in range(0, len(values), 2):
            value = jnp.concatenate([jnp.where(same, v, 0.0) for v in values[at : at + 2]], axis=0)
            where = jnp.concatenate([term] * len(values[at : at + 2]), axis=0)
            parts = split(value, 3)
            out = parts[0].astype(F32)
            for k, (left, _) in enumerate(terms):
                if left:
                    out = jnp.where(where == k, parts[left].astype(F32), out)
            ref[pl.ds(SUB * at, out.shape[0]), :] = out.astype(BF16)

    rows, term, same = spread(NC, ALL, lambda p, i: stoich_ref[p, i])
    products = [rows[p] * rows[q] for p, q in pairs(NX)]
    write(gram_ref, products + [jnp.zeros_like(products[0])], term, same, ALL)
    rows, term, same = spread(NX, ALL, lambda i, p: stoich_ref[p, i])
    write(back_ref, rows, term, same, ALL)
    rows, term, same = spread(NX, MOST, lambda i, p: stoich_ref[p, i])
    write(cross_ref, [rows[i] * rows[j] for i, j in pairs(NC)], term, same, MOST)


def cells_kernel(column_ref, cell_ref, out_ref):
    for y in range(SIDE):
        for kt in range(SUB):
            value = cell_ref[:, pl.ds((y * SUB + kt) * WIN, WIN)]
            for z in range(SIDE):
                out_ref[z * SIDE + y, pl.ds(kt, NC, stride=SUB), :] = value


def cells_to_send(column, cell_state):
    block = SIDE * SUB * WIN
    return pl.pallas_call(
        cells_kernel,
        out_shape=jax.ShapeDtypeStruct((FLOW, NC * SUB, WIN), F32),
        grid_spec=pltpu.PrefetchScalarGridSpec(
            num_scalar_prefetch=1,
            grid=(1,),
            in_specs=[pl.BlockSpec((NC, block), lambda step, column: (0, column[0]))],
            out_specs=pl.BlockSpec((FLOW, NC * SUB, WIN), lambda step, column: (0, 0, 0)),
        ),
        name="cells",
    )(column, cell_state)


def pack_kernel(slot_ref, courant_ref, inflow_ref, pick_ref, message_ref, first_buf, second_buf):
    def rows(ref, buffer, value):
        buffer[...] = jnp.transpose(value)
        even = buffer[pl.ds(0, WIN, stride=2), :]
        odd = buffer[pl.ds(1, WIN, stride=2), :]
        ref[...] = jnp.concatenate([even, odd], axis=1)

    low = jnp.bitwise_and(slot_ref[...], WIN - 1).astype(F32)
    rows(message_ref.at[pl.ds(0, WIN)], first_buf, low)
    rows(message_ref.at[pl.ds(WIN, WIN)], second_buf, courant_ref[...])
    first = inflow_ref[...]
    message_ref[pl.ds(2 * WIN, NC), :] = jnp.concatenate([first, first], axis=1)
    message_ref[pl.ds(2 * WIN + NC, FLOW - NC), :] = jnp.zeros((FLOW - NC, WIN), F32)
    for kt in range(SUB):
        part = jnp.bitwise_and(pick_ref[0, 0, :, pl.ds(kt * WIN, WIN)], WIN - 1)
        message_ref[pl.ds(LANES + kt, FLOW, stride=SUB), :] = part.astype(F32)


def pack(node_slot, courant, inflow, pick):
    return pl.pallas_call(
        pack_kernel,
        out_shape=jax.ShapeDtypeStruct((LANES + WIN, WIN), F32),
        scratch_shapes=[pltpu.VMEM((2 * WIN, HALF), F32)] * 2,
        name="pack",
    )(node_slot.T, courant.T, inflow, pick)


def mean_kernel(sums_ref, out_ref):
    for y in range(SIDE):
        for kt in range(SUB):
            total = sums_ref[y, pl.ds(kt, NQ, stride=SUB), :]
            for z in range(1, SIDE):
                total = total + sums_ref[z * SIDE + y, pl.ds(kt, NQ, stride=SUB), :]
            share = 1.0 / jnp.maximum(total[NQ - 1 :, :], 1.0)
            out_ref[:, pl.ds((y * SUB + kt) * WIN, WIN)] = total[: NQ - 1] * share


def mean(sums):
    return pl.pallas_call(
        mean_kernel,
        out_shape=jax.ShapeDtypeStruct((NQ - 1, SIDE * SUB * WIN), F32),
        name="mean",
    )(sums)


def pairs(order):
    return [(i, j) for i in range(order) for j in range(i + 1)]


def solve_spd(matrix, rhs):
    order = len(rhs)
    lower, inverse, middle = {}, [], []
    for outer in range(order):
        scaled = {}
        for inner in range(outer):
            total = matrix(outer, inner)
            for other in range(inner):
                total = total - scaled[other] * lower[inner, other]
            scaled[inner] = total
            lower[outer, inner] = total * inverse[inner]
        total = matrix(outer, outer)
        value = rhs[outer]
        for other in range(outer):
            total = total - scaled[other] * lower[outer, other]
            value = value - lower[outer, other] * middle[other]
        inverse.append(1.0 / total)
        middle.append(value)
    result = [None] * order
    for outer in reversed(range(order)):
        total = middle[outer] * inverse[outer]
        for other in range(outer + 1, order):
            total = total - lower[other, outer] * result[other]
        result[outer] = total
    return result


def entries(value, diagonal):
    order = len(diagonal)
    at = {pair: SUB * k for k, pair in enumerate(pairs(order))}

    def entry(i, j):
        part = value[at[i, j] : at[i, j] + SUB]
        return part + diagonal[i] if i == j else part

    return entry


def speciate(totals, stoich, logk, gram, cross, back):
    def log_complexes(logfree):
        out = []
        for p in range(NX):
            total = logk(p)
            for i in range(NC):
                total = total + stoich(p, i) * logfree[i]
            out.append(total)
        return out

    def spread(parts):
        taken = dot(back, stack(parts, ALL))
        return [taken[SUB * i : SUB * (i + 1)] for i in range(NC)]

    logfree = [jnp.log(t) for t in totals]
    invfree = [1.0 / t for t in totals]
    weights = dot(gram, stack(split(jnp.concatenate(invfree, axis=0), 3), ALL))
    inverse = [jnp.exp(-jnp.maximum(v, -80.0)) for v in log_complexes(logfree)]
    bound = solve_spd(entries(weights, inverse), [jnp.ones_like(totals[0])] * NX)
    taken = spread(split(jnp.concatenate(bound, axis=0), 3))
    logfree = [x - b * v for x, b, v in zip(logfree, taken, invfree)]
    for sweep in range(ITERS - 1):
        free = [jnp.exp(x) for x in logfree]
        complexes = [jnp.exp(v) for v in log_complexes(logfree)]
        parts = split(jnp.concatenate(complexes, axis=0), 3)
        jacobian = entries(dot(cross, stack(parts, MOST)), free)
        excess = [(t - f) - b for t, f, b in zip(totals, free, spread(parts))]
        logfree = [x + d for x, d in zip(logfree, solve_spd(jacobian, excess))]
    return [jnp.exp(x) for x in logfree] + [jnp.exp(v) for v in log_complexes(logfree)]


def react_kernel(
    recv_ref, lanes_ref, message_ref, stoich_ref, logk_ref,
    out_ref, coef, carry, rows_buf, gram_ref, cross_ref, back_ref,
):
    build_tables(stoich_ref, gram_ref, cross_ref, back_ref)
    lane = lax.broadcasted_iota(jnp.int32, (SUB, WIN), 1)
    row = lax.broadcasted_iota(jnp.int32, (SUB, WIN), 0)
    cell = lax.broadcasted_iota(jnp.int32, (WIN, WIN), 0)
    odd = lane >= HALF
    for p in range(NX):
        for i in range(NC):
            coef[p * NC + i] = jnp.full((SUB, WIN), stoich_ref[p, i], F32)
        coef[NX * NC + p] = jnp.full((SUB, WIN), logk_ref[p], F32)
    rows_buf[...] = jnp.zeros(rows_buf.shape, F32)
    for b in range(BATCH):
        rows_buf[pl.ds(b * SUB * PAD + NQ - 1, SUB, stride=PAD), :] = jnp.ones((SUB, WIN), F32)
    for c in range(NC):
        carry[c] = jnp.broadcast_to(message_ref[pl.ds(2 * WIN + c, 1), :], (SUB, WIN))

    def swap(value):
        return pltpu.roll(value, HALF, 1)

    def wide(value):
        return jnp.concatenate([value] * BATCH, axis=1)

    def step(index, unused):
        moved = [[] for _ in range(NC)]
        places = []
        for b in range(BATCH):
            source = index * BATCH + b
            base = pl.multiple_of(source * SUB, SUB)
            slot = message_ref[pl.ds(base, SUB), :].astype(jnp.int32)
            local = jnp.take_along_axis(lanes_ref[source], slot, axis=1).astype(jnp.int32)
            places.append(local)
            courant = message_ref[pl.ds(base + WIN, SUB), :]
            ratio = 1.0 / (1.0 + courant)
            weight = courant * ratio
            pair = jnp.where(odd, weight * swap(weight), weight)
            run = jnp.where(odd, pair, swap(pair))
            factors = []
            for reach in (1, 2, 4):
                factors.append(jnp.where(row >= reach, run, 0.0))
                run = run * jnp.where(row >= reach, pltpu.roll(run, reach, 0), 1.0)
            for c in range(NC):
                part = jnp.take_along_axis(recv_ref[source, pl.ds(SUB * c, SUB), :], local, axis=1) * ratio
                part = jnp.where(odd, weight * swap(part) + part, part)
                total = jnp.where(odd, part, swap(part))
                for level, reach in enumerate((1, 2, 4)):
                    total = total + factors[level] * pltpu.roll(total, reach, 0)
                before = carry[c]
                total = total + run * before
                carry[c] = jnp.broadcast_to(total[SUB - 1 :, :], (SUB, WIN))
                ahead = jnp.where(row == 0, before, pltpu.roll(total, 1, 0))
                moved[c].append(part + pair * ahead)
        species = speciate(
            [jnp.concatenate(parts, axis=1) for parts in moved],
            lambda p, i: wide(coef[p * NC + i]),
            lambda p: wide(coef[NX * NC + p]),
            gram_ref[:168],
            cross_ref[...],
            back_ref[...],
        )
        for q in range(NC + NX):
            for b in range(BATCH):
                rows_buf[pl.ds(b * SUB * PAD + q, SUB, stride=PAD), :] = species[q][
                    :, b * WIN : (b + 1) * WIN
                ]
        for b in range(BATCH):
            for kt in range(SUB):
                hot = (cell == jnp.broadcast_to(places[b][kt : kt + 1, :], (WIN, WIN))).astype(BF16)
                value = rows_buf[pl.ds((b * SUB + kt) * PAD, PAD), :]
                both = lax.dot_general(
                    jnp.concatenate(split(value, 2), axis=0),
                    hot,
                    (((1,), (1,)), ((), ())),
                    preferred_element_type=F32,
                )
                sums = both[:PAD] + both[PAD:]
                out_ref[index * BATCH + b, pl.ds(kt, NQ, stride=SUB), :] = sums[:NQ]
        return unused

    lax.fori_loop(0, FLOW // BATCH, step, 0)


def react(recv, lanes, message, stoich, logk):
    return pl.pallas_call(
        react_kernel,
        out_shape=jax.ShapeDtypeStruct((FLOW, NQ * SUB, WIN), F32),
        in_specs=[pl.BlockSpec(memory_space=pltpu.VMEM)] * 3
        + [pl.BlockSpec(memory_space=pltpu.SMEM)] * 2,
        scratch_shapes=[
            pltpu.VMEM((NX * NC + NX, SUB, WIN), F32),
            pltpu.VMEM((NC, SUB, WIN), F32),
            pltpu.VMEM((BATCH * SUB * PAD, WIN), F32),
            pltpu.VMEM((176, len(ALL) * NC * SUB), BF16),
            pltpu.VMEM((624, len(MOST) * NX * SUB), BF16),
            pltpu.VMEM((96, len(ALL) * NX * SUB), BF16),
        ],
        compiler_params=pltpu.CompilerParams(vmem_limit_bytes=48 * 1024 * 1024),
        name="react",
    )(recv, lanes, message, stoich, logk)


def body(cell_state, inflow, courant, pick, node_slot, stoich, logk):
    everywhere = ("z", "y", "h", "q")
    column = lax.axis_index("h") * SIDE + lax.axis_index("q")
    route = []
    for z in range(SIDE):
        for y in range(SIDE):
            for x in range(SIDE):
                for h in range(2):
                    source = (z * SIDE + y) * 2 * SIDE + x * 2 + h
                    route.append((source, (x * SIDE + y) * 2 * SIDE + h * SIDE + z))
    send = cells_to_send(column[None], cell_state)
    recv = lax.all_to_all(send, ("z", "y"), 0, 0, tiled=True)
    message = lax.ppermute(pack(node_slot, courant, inflow, pick), everywhere, route)
    lanes = message[LANES:].reshape(FLOW, SUB, WIN)
    recv, lanes = lax.optimization_barrier((recv, lanes))
    lanes = lax.all_to_all(lanes, ("q", "y"), 0, 0, tiled=True)
    sums = react(recv, lanes, message, stoich, logk)
    back = lax.all_to_all(sums, ("z", "y"), 0, 0, tiled=True)
    return mean(back)


def solution(mesh):
    grid = Mesh(mesh.devices.reshape(SIDE, SIDE, 2, SIDE), ("z", "y", "h", "q"))
    flow, group = ("z", "y"), ("h", "q")
    every = P(None, flow + group)
    placed = (P(None, flow), every, every, P(group, flow, None, None), every, P(), P())
    return jax.shard_map(body, mesh=grid, in_specs=placed, out_specs=every, check_vma=False)
```

```python
import functools

import jax
import jax.numpy as jnp
from jax import lax
from jax.experimental import pallas as pl
from jax.experimental.pallas import tpu as pltpu
from jax.sharding import Mesh, PartitionSpec as P

ITERS = 4
WIN = 128
NC = 12
NX = 6
NQ = NC + NX + 1
PAD = 24
SIDE = 4
FLOW = 16
SUB = 8
HALF = 64
LANES = 2 * WIN + FLOW
BATCH = 8
BF16 = jnp.bfloat16
F32 = jnp.float32


def split(value, parts):
    out = []
    for part in range(parts):
        out.append(value.astype(BF16))
        if part < parts - 1:
            value = value - out[-1].astype(F32)
    return out


def dot(left, right):
    return jnp.dot(left, right, preferred_element_type=F32)


ALL = [(0, 0), (0, 1), (0, 2), (1, 0), (1, 1), (2, 0)]
MOST = ALL[:5]


def stack(parts, terms):
    return jnp.concatenate([parts[right] for _, right in terms], axis=0)


def build_tables(stoich_ref, gram_ref, cross_ref, back_ref):
    def spread(count, terms, pick):
        lane = lax.broadcasted_iota(jnp.int32, (SUB, len(terms) * count * SUB), 1)
        row = lax.broadcasted_iota(jnp.int32, lane.shape, 0)
        which = lane % (count * SUB) // SUB
        vectors = []
        for outer in range(NC + NX - count):
            value = jnp.zeros(lane.shape, F32)
            for inner in range(count):
                value = jnp.where(which == inner, pick(outer, inner), value)
            vectors.append(value)
        return vectors, lane // (count * SUB), lane % SUB == row

    def write(ref, values, term, same, terms):
        for at in range(0, len(values), 2):
            value = jnp.concatenate([jnp.where(same, v, 0.0) for v in values[at : at + 2]], axis=0)
            where = jnp.concatenate([term] * len(values[at : at + 2]), axis=0)
            parts = split(value, 3)
            out = parts[0].astype(F32)
            for k, (left, _) in enumerate(terms):
                if left:
                    out = jnp.where(where == k, parts[left].astype(F32), out)
            ref[pl.ds(SUB * at, out.shape[0]), :] = out.astype(BF16)

    rows, term, same = spread(NC, ALL, lambda p, i: stoich_ref[p, i])
    products = [rows[p] * rows[q] for p, q in pairs(NX)]
    write(gram_ref, products + [jnp.zeros_like(products[0])], term, same, ALL)
    rows, term, same = spread(NX, ALL, lambda i, p: stoich_ref[p, i])
    write(back_ref, rows, term, same, ALL)
    rows, term, same = spread(NX, MOST, lambda i, p: stoich_ref[p, i])
    write(cross_ref, [rows[i] * rows[j] for i, j in pairs(NC)], term, same, MOST)


def cells_kernel(column_ref, cell_ref, pick_ref, out_ref):
    for y in range(SIDE):
        for kt in range(SUB):
            value = cell_ref[:, pl.ds((y * SUB + kt) * WIN, WIN)]
            for z in range(SIDE):
                out_ref[z * SIDE + y, pl.ds(kt, NC, stride=SUB), :] = value
    for kt in range(SUB):
        lanes = jnp.bitwise_and(pick_ref[0, 0, :, pl.ds(kt * WIN, WIN)], WIN - 1).astype(F32)
        for b in range(FLOW):
            out_ref[b, pl.ds(NC * SUB + kt, 1), :] = lanes[b : b + 1, :]


def cells_to_send(column, cell_state, pick):
    block = SIDE * SUB * WIN
    return pl.pallas_call(
        cells_kernel,
        out_shape=jax.ShapeDtypeStruct((FLOW, (NC + 1) * SUB, WIN), F32),
        grid_spec=pltpu.PrefetchScalarGridSpec(
            num_scalar_prefetch=1,
            grid=(1,),
            in_specs=[
                pl.BlockSpec((NC, block), lambda step, column: (0, column[0])),
                pl.BlockSpec((1, 1, FLOW, SUB * WIN), lambda step, column: (0, 0, 0, 0)),
            ],
            out_specs=pl.BlockSpec((FLOW, (NC + 1) * SUB, WIN), lambda step, column: (0, 0, 0)),
        ),
        name="cells",
    )(column, cell_state, pick)


def locate_kernel(recv_ref, packed_ref, message_ref):
    for source in range(FLOW):
        rows = pl.ds(source * SUB, SUB)
        lane = recv_ref[source, pl.ds(NC * SUB, SUB), :]
        message_ref[rows, :] = jnp.take_along_axis(lane, packed_ref[rows, :].astype(jnp.int32), axis=1)
    rest = pl.ds(WIN, LANES - WIN)
    message_ref[rest, :] = packed_ref[rest, :]


def locate(recv, packed):
    return pl.pallas_call(
        locate_kernel,
        out_shape=jax.ShapeDtypeStruct(packed.shape, F32),
        in_specs=[pl.BlockSpec(memory_space=pltpu.VMEM)] * 2,
        compiler_params=pltpu.CompilerParams(vmem_limit_bytes=8 * 1024 * 1024),
        name="locate",
    )(recv, packed)


def pack_kernel(slot_ref, courant_ref, inflow_ref, message_ref, first_buf, second_buf):
    def rows(ref, buffer, value):
        buffer[...] = jnp.transpose(value)
        even = buffer[pl.ds(0, WIN, stride=2), :]
        odd = buffer[pl.ds(1, WIN, stride=2), :]
        ref[...] = jnp.concatenate([even, odd], axis=1)

    low = jnp.bitwise_and(slot_ref[...], WIN - 1).astype(F32)
    rows(message_ref.at[pl.ds(0, WIN)], first_buf, low)
    rows(message_ref.at[pl.ds(WIN, WIN)], second_buf, courant_ref[...])
    first = inflow_ref[...]
    message_ref[pl.ds(2 * WIN, NC), :] = jnp.concatenate([first, first], axis=1)
    message_ref[pl.ds(2 * WIN + NC, FLOW - NC), :] = jnp.zeros((FLOW - NC, WIN), F32)


def pack(node_slot, courant, inflow):
    return pl.pallas_call(
        pack_kernel,
        out_shape=jax.ShapeDtypeStruct((LANES, WIN), F32),
        in_specs=[pl.BlockSpec(memory_space=pltpu.VMEM)] * 3,
        scratch_shapes=[pltpu.VMEM((2 * WIN, HALF), F32)] * 2,
        compiler_params=pltpu.CompilerParams(vmem_limit_bytes=8 * 1024 * 1024),
        name="pack",
    )(node_slot.T, courant.T, inflow)


def mean_kernel(sums_ref, out_ref):
    for y in range(SIDE):
        for kt in range(SUB):
            total = sums_ref[y, pl.ds(kt, NQ, stride=SUB), :]
            for z in range(1, SIDE):
                total = total + sums_ref[z * SIDE + y, pl.ds(kt, NQ, stride=SUB), :]
            share = 1.0 / jnp.maximum(total[NQ - 1 :, :], 1.0)
            out_ref[:, pl.ds((y * SUB + kt) * WIN, WIN)] = total[: NQ - 1] * share


def mean(sums):
    return pl.pallas_call(
        mean_kernel,
        out_shape=jax.ShapeDtypeStruct((NQ - 1, SIDE * SUB * WIN), F32),
        in_specs=[pl.BlockSpec(memory_space=pltpu.VMEM)],
        compiler_params=pltpu.CompilerParams(vmem_limit_bytes=8 * 1024 * 1024),
        name="mean",
    )(sums)


def pairs(order):
    return [(i, j) for i in range(order) for j in range(i + 1)]


def solve_spd(matrix, rhs):
    order = len(rhs)
    lower, inverse, middle = {}, [], []
    for outer in range(order):
        scaled = {}
        for inner in range(outer):
            total = matrix(outer, inner)
            for other in range(inner):
                total = total - scaled[other] * lower[inner, other]
            scaled[inner] = total
            lower[outer, inner] = total * inverse[inner]
        total = matrix(outer, outer)
        value = rhs[outer]
        for other in range(outer):
            total = total - scaled[other] * lower[outer, other]
            value = value - lower[outer, other] * middle[other]
        inverse.append(1.0 / total)
        middle.append(value)
    result = [None] * order
    for outer in reversed(range(order)):
        total = middle[outer] * inverse[outer]
        for other in range(outer + 1, order):
            total = total - lower[other, outer] * result[other]
        result[outer] = total
    return result


def entries(value, diagonal):
    order = len(diagonal)
    at = {pair: SUB * k for k, pair in enumerate(pairs(order))}

    def entry(i, j):
        part = value[at[i, j] : at[i, j] + SUB]
        return part + diagonal[i] if i == j else part

    return entry


def speciate(totals, stoich, logk, gram, cross, back):
    def log_complexes(logfree):
        out = []
        for p in range(NX):
            total = logk(p)
            for i in range(NC):
                total = total + stoich(p, i) * logfree[i]
            out.append(total)
        return out

    def spread(parts):
        taken = dot(back, stack(parts, ALL))
        return [taken[SUB * i : SUB * (i + 1)] for i in range(NC)]

    logfree = [jnp.log(t) for t in totals]
    invfree = [1.0 / t for t in totals]
    weights = dot(gram, stack(split(jnp.concatenate(invfree, axis=0), 3), ALL))
    inverse = [jnp.exp(-jnp.maximum(v, -80.0)) for v in log_complexes(logfree)]
    bound = solve_spd(entries(weights, inverse), [jnp.ones_like(totals[0])] * NX)
    taken = spread(split(jnp.concatenate(bound, axis=0), 3))
    logfree = [x - b * v for x, b, v in zip(logfree, taken, invfree)]
    for sweep in range(ITERS - 1):
        free = [jnp.exp(x) for x in logfree]
        complexes = [jnp.exp(v) for v in log_complexes(logfree)]
        parts = split(jnp.concatenate(complexes, axis=0), 3)
        jacobian = entries(dot(cross, stack(parts, MOST)), free)
        excess = [(t - f) - b for t, f, b in zip(totals, free, spread(parts))]
        logfree = [x + d for x, d in zip(logfree, solve_spd(jacobian, excess))]
    return [jnp.exp(x) for x in logfree] + [jnp.exp(v) for v in log_complexes(logfree)]


def react_kernel(
    recv_ref, message_ref, stoich_ref, logk_ref,
    out_ref, coef, carry, rows_buf, gram_ref, cross_ref, back_ref,
):
    build_tables(stoich_ref, gram_ref, cross_ref, back_ref)
    lane = lax.broadcasted_iota(jnp.int32, (SUB, WIN), 1)
    row = lax.broadcasted_iota(jnp.int32, (SUB, WIN), 0)
    cell = lax.broadcasted_iota(jnp.int32, (WIN, WIN), 0)
    odd = lane >= HALF
    for p in range(NX):
        for i in range(NC):
            coef[p * NC + i] = jnp.full((SUB, WIN), stoich_ref[p, i], F32)
        coef[NX * NC + p] = jnp.full((SUB, WIN), logk_ref[p], F32)
    rows_buf[...] = jnp.zeros(rows_buf.shape, F32)
    for b in range(BATCH):
        rows_buf[pl.ds(b * SUB * PAD + NQ - 1, SUB, stride=PAD), :] = jnp.ones((SUB, WIN), F32)
    for c in range(NC):
        carry[c] = jnp.broadcast_to(message_ref[pl.ds(2 * WIN + c, 1), :], (SUB, WIN))

    def swap(value):
        return pltpu.roll(value, HALF, 1)

    def wide(value):
        return jnp.concatenate([value] * BATCH, axis=1)

    def step(index, unused):
        moved = [[] for _ in range(NC)]
        places = []
        for b in range(BATCH):
            source = index * BATCH + b
            base = pl.multiple_of(source * SUB, SUB)
            local = message_ref[pl.ds(base, SUB), :].astype(jnp.int32)
            places.append(local)
            courant = message_ref[pl.ds(base + WIN, SUB), :]
            ratio = 1.0 / (1.0 + courant)
            weight = courant * ratio
            pair = jnp.where(odd, weight * swap(weight), weight)
            run = jnp.where(odd, pair, swap(pair))
            factors = []
            for reach in (1, 2, 4):
                factors.append(jnp.where(row >= reach, run, 0.0))
                run = run * jnp.where(row >= reach, pltpu.roll(run, reach, 0), 1.0)
            for c in range(NC):
                part = jnp.take_along_axis(recv_ref[source, pl.ds(SUB * c, SUB), :], local, axis=1) * ratio
                part = jnp.where(odd, weight * swap(part) + part, part)
                total = jnp.where(odd, part, swap(part))
                for level, reach in enumerate((1, 2, 4)):
                    total = total + factors[level] * pltpu.roll(total, reach, 0)
                before = carry[c]
                total = total + run * before
                carry[c] = jnp.broadcast_to(total[SUB - 1 :, :], (SUB, WIN))
                ahead = jnp.where(row == 0, before, pltpu.roll(total, 1, 0))
                moved[c].append(part + pair * ahead)
        species = speciate(
            [jnp.concatenate(parts, axis=1) for parts in moved],
            lambda p, i: wide(coef[p * NC + i]),
            lambda p: wide(coef[NX * NC + p]),
            gram_ref[:168],
            cross_ref[...],
            back_ref[...],
        )
        for q in range(NC + NX):
            for b in range(BATCH):
                rows_buf[pl.ds(b * SUB * PAD + q, SUB, stride=PAD), :] = species[q][
                    :, b * WIN : (b + 1) * WIN
                ]
        for b in range(BATCH):
            for kt in range(SUB):
                hot = (cell == jnp.broadcast_to(places[b][kt : kt + 1, :], (WIN, WIN))).astype(BF16)
                value = rows_buf[pl.ds((b * SUB + kt) * PAD, PAD), :]
                both = lax.dot_general(
                    jnp.concatenate(split(value, 2), axis=0),
                    hot,
                    (((1,), (1,)), ((), ())),
                    preferred_element_type=F32,
                )
                sums = both[:PAD] + both[PAD:]
                out_ref[index * BATCH + b, pl.ds(kt, NQ, stride=SUB), :] = sums[:NQ]
        return unused

    lax.fori_loop(0, FLOW // BATCH, step, 0)


def react(recv, message, stoich, logk):
    return pl.pallas_call(
        react_kernel,
        out_shape=jax.ShapeDtypeStruct((FLOW, NQ * SUB, WIN), F32),
        in_specs=[pl.BlockSpec(memory_space=pltpu.VMEM)] * 2
        + [pl.BlockSpec(memory_space=pltpu.SMEM)] * 2,
        scratch_shapes=[
            pltpu.VMEM((NX * NC + NX, SUB, WIN), F32),
            pltpu.VMEM((NC, SUB, WIN), F32),
            pltpu.VMEM((BATCH * SUB * PAD, WIN), F32),
            pltpu.VMEM((176, len(ALL) * NC * SUB), BF16),
            pltpu.VMEM((624, len(MOST) * NX * SUB), BF16),
            pltpu.VMEM((96, len(ALL) * NX * SUB), BF16),
        ],
        compiler_params=pltpu.CompilerParams(vmem_limit_bytes=24 * 1024 * 1024),
        name="react",
    )(recv, message, stoich, logk)


def body(cell_state, inflow, courant, pick, node_slot, stoich, logk):
    everywhere = ("z", "y", "h", "q")
    column = lax.axis_index("h") * SIDE + lax.axis_index("q")
    route = []
    for z in range(SIDE):
        for y in range(SIDE):
            for x in range(SIDE):
                for h in range(2):
                    source = (z * SIDE + y) * 2 * SIDE + x * 2 + h
                    route.append((source, (x * SIDE + y) * 2 * SIDE + h * SIDE + z))
    send = cells_to_send(column[None], cell_state, pick)
    recv = lax.all_to_all(send, ("z", "y"), 0, 0, tiled=True)
    packed = pack(node_slot, courant, inflow)
    message = lax.ppermute(locate(recv, packed), everywhere, route)
    sums = react(recv, message, stoich, logk)
    back = lax.all_to_all(sums, ("z", "y"), 0, 0, tiled=True)
    return mean(back)


def solution(mesh):
    grid = Mesh(mesh.devices.reshape(SIDE, SIDE, 2, SIDE), ("z", "y", "h", "q"))
    flow, group = ("z", "y"), ("h", "q")
    every = P(None, flow + group)
    placed = (P(None, flow), every, every, P(group, flow, None, None), every, P(), P())
    return jax.shard_map(body, mesh=grid, in_specs=placed, out_specs=every, check_vma=False)
```

```python
import functools

import jax
import jax.numpy as jnp
from jax import lax
from jax.experimental import pallas as pl
from jax.experimental.pallas import tpu as pltpu
from jax.sharding import Mesh, PartitionSpec as P

ITERS = 4
WIN = 128
NC = 12
NX = 6
NQ = NC + NX + 1
PAD = 24
SIDE = 4
FLOW = 16
SUB = 8
HALF = 64
LANES = 2 * WIN + FLOW
BATCH = 8
BF16 = jnp.bfloat16
F32 = jnp.float32


def split(value, parts):
    out = []
    for part in range(parts):
        out.append(value.astype(BF16))
        if part < parts - 1:
            value = value - out[-1].astype(F32)
    return out


def dot(left, right):
    return jnp.dot(left, right, preferred_element_type=F32)


ALL = [(0, 0), (0, 1), (0, 2), (1, 0), (1, 1), (2, 0)]
MOST = ALL[:5]


def stack(parts, terms):
    return jnp.concatenate([parts[right] for _, right in terms], axis=0)


def build_tables(stoich_ref, gram_ref, cross_ref, back_ref):
    def spread(count, terms, pick):
        lane = lax.broadcasted_iota(jnp.int32, (SUB, len(terms) * count * SUB), 1)
        row = lax.broadcasted_iota(jnp.int32, lane.shape, 0)
        which = lane % (count * SUB) // SUB
        vectors = []
        for outer in range(NC + NX - count):
            value = jnp.zeros(lane.shape, F32)
            for inner in range(count):
                value = jnp.where(which == inner, pick(outer, inner), value)
            vectors.append(value)
        return vectors, lane // (count * SUB), lane % SUB == row

    def write(ref, values, term, same, terms):
        for at in range(0, len(values), 2):
            value = jnp.concatenate([jnp.where(same, v, 0.0) for v in values[at : at + 2]], axis=0)
            where = jnp.concatenate([term] * len(values[at : at + 2]), axis=0)
            parts = split(value, 3)
            out = parts[0].astype(F32)
            for k, (left, _) in enumerate(terms):
                if left:
                    out = jnp.where(where == k, parts[left].astype(F32), out)
            ref[pl.ds(SUB * at, out.shape[0]), :] = out.astype(BF16)

    rows, term, same = spread(NC, ALL, lambda p, i: stoich_ref[p, i])
    products = [rows[p] * rows[q] for p, q in pairs(NX)]
    write(gram_ref, products + [jnp.zeros_like(products[0])], term, same, ALL)
    rows, term, same = spread(NX, ALL, lambda i, p: stoich_ref[p, i])
    write(back_ref, rows, term, same, ALL)
    rows, term, same = spread(NX, MOST, lambda i, p: stoich_ref[p, i])
    write(cross_ref, [rows[i] * rows[j] for i, j in pairs(NC)], term, same, MOST)


def cells_kernel(column_ref, cell_ref, pick_ref, out_ref):
    for y in range(SIDE):
        for kt in range(SUB):
            value = cell_ref[:, pl.ds((y * SUB + kt) * WIN, WIN)]
            for z in range(SIDE):
                out_ref[z * SIDE + y, pl.ds(kt, NC, stride=SUB), :] = value
    for kt in range(SUB):
        lanes = jnp.bitwise_and(pick_ref[0, 0, :, pl.ds(kt * WIN, WIN)], WIN - 1).astype(F32)
        for b in range(FLOW):
            out_ref[b, pl.ds(NC * SUB + kt, 1), :] = lanes[b : b + 1, :]


def cells_to_send(column, cell_state, pick):
    block = SIDE * SUB * WIN
    return pl.pallas_call(
        cells_kernel,
        out_shape=jax.ShapeDtypeStruct((FLOW, (NC + 1) * SUB, WIN), F32),
        grid_spec=pltpu.PrefetchScalarGridSpec(
            num_scalar_prefetch=1,
            grid=(1,),
            in_specs=[
                pl.BlockSpec((NC, block), lambda step, column: (0, column[0])),
                pl.BlockSpec((1, 1, FLOW, SUB * WIN), lambda step, column: (0, 0, 0, 0)),
            ],
            out_specs=pl.BlockSpec((FLOW, (NC + 1) * SUB, WIN), lambda step, column: (0, 0, 0)),
        ),
        name="cells",
    )(column, cell_state, pick)


def locate_kernel(recv_ref, slots_ref, lanes_ref):
    for source in range(FLOW):
        rows = pl.ds(source * SUB, SUB)
        lane = recv_ref[source, pl.ds(NC * SUB, SUB), :]
        lanes_ref[rows, :] = jnp.take_along_axis(lane, slots_ref[rows, :], axis=1)


def locate(recv, slots):
    return pl.pallas_call(
        locate_kernel,
        out_shape=jax.ShapeDtypeStruct(slots.shape, F32),
        in_specs=[pl.BlockSpec(memory_space=pltpu.VMEM)] * 2,
        compiler_params=pltpu.CompilerParams(vmem_limit_bytes=8 * 1024 * 1024),
        name="locate",
    )(recv, slots)


def pack_kernel(slot_ref, courant_ref, inflow_ref, slots_ref, message_ref, first_buf, second_buf):
    def rows(ref, buffer, value):
        buffer[...] = jnp.transpose(value)
        even = buffer[pl.ds(0, WIN, stride=2), :]
        odd = buffer[pl.ds(1, WIN, stride=2), :]
        ref[...] = jnp.concatenate([even, odd], axis=1)

    rows(slots_ref, first_buf, jnp.bitwise_and(slot_ref[...], WIN - 1))
    rows(message_ref.at[pl.ds(0, WIN)], second_buf, courant_ref[...])
    first = inflow_ref[...]
    message_ref[pl.ds(WIN, NC), :] = jnp.concatenate([first, first], axis=1)
    message_ref[pl.ds(WIN + NC, FLOW - NC), :] = jnp.zeros((FLOW - NC, WIN), F32)


def pack(node_slot, courant, inflow):
    return pl.pallas_call(
        pack_kernel,
        out_shape=(
            jax.ShapeDtypeStruct((WIN, WIN), jnp.int32),
            jax.ShapeDtypeStruct((WIN + FLOW, WIN), F32),
        ),
        in_specs=[pl.BlockSpec(memory_space=pltpu.VMEM)] * 3,
        scratch_shapes=[
            pltpu.VMEM((2 * WIN, HALF), jnp.int32),
            pltpu.VMEM((2 * WIN, HALF), F32),
        ],
        compiler_params=pltpu.CompilerParams(vmem_limit_bytes=8 * 1024 * 1024),
        name="pack",
    )(node_slot.T, courant.T, inflow)


def mean_kernel(sums_ref, out_ref):
    for y in range(SIDE):
        for kt in range(SUB):
            total = sums_ref[y, pl.ds(kt, NQ, stride=SUB), :]
            for z in range(1, SIDE):
                total = total + sums_ref[z * SIDE + y, pl.ds(kt, NQ, stride=SUB), :]
            share = 1.0 / jnp.maximum(total[NQ - 1 :, :], 1.0)
            out_ref[:, pl.ds((y * SUB + kt) * WIN, WIN)] = total[: NQ - 1] * share


def mean(sums):
    return pl.pallas_call(
        mean_kernel,
        out_shape=jax.ShapeDtypeStruct((NQ - 1, SIDE * SUB * WIN), F32),
        in_specs=[pl.BlockSpec(memory_space=pltpu.VMEM)],
        compiler_params=pltpu.CompilerParams(vmem_limit_bytes=8 * 1024 * 1024),
        name="mean",
    )(sums)


def pairs(order):
    return [(i, j) for i in range(order) for j in range(i + 1)]


def solve_spd(matrix, rhs):
    order = len(rhs)
    lower, inverse, middle = {}, [], []
    for outer in range(order):
        scaled = {}
        for inner in range(outer):
            total = matrix(outer, inner)
            for other in range(inner):
                total = total - scaled[other] * lower[inner, other]
            scaled[inner] = total
            lower[outer, inner] = total * inverse[inner]
        total = matrix(outer, outer)
        value = rhs[outer]
        for other in range(outer):
            total = total - scaled[other] * lower[outer, other]
            value = value - lower[outer, other] * middle[other]
        inverse.append(1.0 / total)
        middle.append(value)
    result = [None] * order
    for outer in reversed(range(order)):
        total = middle[outer] * inverse[outer]
        for other in range(outer + 1, order):
            total = total - lower[other, outer] * result[other]
        result[outer] = total
    return result


def entries(value, diagonal):
    order = len(diagonal)
    at = {pair: SUB * k for k, pair in enumerate(pairs(order))}

    def entry(i, j):
        part = value[at[i, j] : at[i, j] + SUB]
        return part + diagonal[i] if i == j else part

    return entry


def speciate(totals, stoich, logk, gram, cross, back):
    def log_complexes(logfree):
        out = []
        for p in range(NX):
            total = logk(p)
            for i in range(NC):
                total = total + stoich(p, i) * logfree[i]
            out.append(total)
        return out

    def spread(parts):
        taken = dot(back, stack(parts, ALL))
        return [taken[SUB * i : SUB * (i + 1)] for i in range(NC)]

    logfree = [jnp.log(t) for t in totals]
    invfree = [1.0 / t for t in totals]
    weights = dot(gram, stack(split(jnp.concatenate(invfree, axis=0), 3), ALL))
    logc = log_complexes(logfree)
    inverse = [jnp.exp(-jnp.maximum(v, -80.0)) for v in logc]
    bound = solve_spd(entries(weights, inverse), [jnp.ones_like(totals[0])] * NX)
    taken = spread(split(jnp.concatenate(bound, axis=0), 3))
    logfree = [x - b * v for x, b, v in zip(logfree, taken, invfree)]
    logc = [v + (b * e - 1.0) for v, b, e in zip(logc, bound, inverse)]
    for sweep in range(ITERS - 1):
        free = [jnp.exp(x) for x in logfree]
        if sweep:
            logc = log_complexes(logfree)
        complexes = [jnp.exp(v) for v in logc]
        parts = split(jnp.concatenate(complexes, axis=0), 3)
        jacobian = entries(dot(cross, stack(parts, MOST)), free)
        excess = [(t - f) - b for t, f, b in zip(totals, free, spread(parts))]
        logfree = [x + d for x, d in zip(logfree, solve_spd(jacobian, excess))]
    return [jnp.exp(x) for x in logfree] + [jnp.exp(v) for v in log_complexes(logfree)]


def react_kernel(
    recv_ref, lanes_ref, message_ref, stoich_ref, logk_ref,
    out_ref, coef, carry, rows_buf, gram_ref, cross_ref, back_ref,
):
    build_tables(stoich_ref, gram_ref, cross_ref, back_ref)
    lane = lax.broadcasted_iota(jnp.int32, (SUB, WIN), 1)
    row = lax.broadcasted_iota(jnp.int32, (SUB, WIN), 0)
    cell = lax.broadcasted_iota(jnp.int32, (WIN, WIN), 0)
    odd = lane >= HALF
    none = jnp.zeros((WIN, WIN), BF16)
    for p in range(NX):
        for i in range(NC):
            coef[p * NC + i] = jnp.full((SUB, WIN), stoich_ref[p, i], F32)
        coef[NX * NC + p] = jnp.full((SUB, WIN), logk_ref[p], F32)
    rows_buf[...] = jnp.zeros(rows_buf.shape, F32)
    for b in range(BATCH):
        rows_buf[pl.ds(b * SUB * PAD + NQ - 1, SUB, stride=PAD), :] = jnp.ones((SUB, WIN), F32)
    for c in range(NC):
        carry[c] = jnp.broadcast_to(message_ref[pl.ds(WIN + c, 1), :], (SUB, WIN))

    def swap(value):
        return pltpu.roll(value, HALF, 1)

    def wide(value):
        return jnp.concatenate([value] * BATCH, axis=1)

    def step(index, unused):
        moved = [[] for _ in range(NC)]
        places = []
        for b in range(BATCH):
            source = index * BATCH + b
            base = pl.multiple_of(source * SUB, SUB)
            local = lanes_ref[pl.ds(base, SUB), :].astype(jnp.int32)
            places.append(local)
            courant = message_ref[pl.ds(base, SUB), :]
            ratio = 1.0 / (1.0 + courant)
            weight = courant * ratio
            pair = jnp.where(odd, weight * swap(weight), weight)
            run = jnp.where(odd, pair, swap(pair))
            factors = []
            for reach in (1, 2, 4):
                factors.append(jnp.where(row >= reach, run, 0.0))
                run = run * jnp.where(row >= reach, pltpu.roll(run, reach, 0), 1.0)
            for c in range(NC):
                part = jnp.take_along_axis(recv_ref[source, pl.ds(SUB * c, SUB), :], local, axis=1) * ratio
                part = jnp.where(odd, weight * swap(part) + part, part)
                total = jnp.where(odd, part, swap(part))
                for level, reach in enumerate((1, 2, 4)):
                    total = total + factors[level] * pltpu.roll(total, reach, 0)
                before = carry[c]
                total = total + run * before
                carry[c] = jnp.broadcast_to(total[SUB - 1 :, :], (SUB, WIN))
                ahead = jnp.where(row == 0, before, pltpu.roll(total, 1, 0))
                moved[c].append(part + pair * ahead)
        species = speciate(
            [jnp.concatenate(parts, axis=1) for parts in moved],
            lambda p, i: wide(coef[p * NC + i]),
            lambda p: wide(coef[NX * NC + p]),
            gram_ref[:168],
            cross_ref[...],
            back_ref[...],
        )
        for q in range(NC + NX):
            for b in range(BATCH):
                rows_buf[pl.ds(b * SUB * PAD + q, SUB, stride=PAD), :] = species[q][
                    :, b * WIN : (b + 1) * WIN
                ]
        for b in range(BATCH):
            for kt in range(0, SUB, 2):
                hots, values = [], []
                for k in (kt, kt + 1):
                    place = jnp.broadcast_to(places[b][k : k + 1, :], (WIN, WIN))
                    hots.append((cell == place).astype(BF16))
                    value = rows_buf[pl.ds((b * SUB + k) * PAD, PAD), :]
                    values.append(jnp.concatenate(split(value, 2), axis=0))
                upper = jnp.concatenate([hots[0], none], axis=1)
                hot = jnp.concatenate([upper, jnp.concatenate([none, hots[1]], axis=1)], axis=0)
                both = lax.dot_general(
                    jnp.concatenate(values, axis=1),
                    hot,
                    (((1,), (1,)), ((), ())),
                    preferred_element_type=F32,
                )
                sums = both[:PAD] + both[PAD:]
                for k in (0, 1):
                    part = sums[:NQ, k * WIN : (k + 1) * WIN]
                    out_ref[index * BATCH + b, pl.ds(kt + k, NQ, stride=SUB), :] = part
        return unused

    lax.fori_loop(0, FLOW // BATCH, step, 0)


def react(recv, lanes, message, stoich, logk):
    return pl.pallas_call(
        react_kernel,
        out_shape=jax.ShapeDtypeStruct((FLOW, NQ * SUB, WIN), F32),
        in_specs=[pl.BlockSpec(memory_space=pltpu.VMEM)] * 3
        + [pl.BlockSpec(memory_space=pltpu.SMEM)] * 2,
        scratch_shapes=[
            pltpu.VMEM((NX * NC + NX, SUB, WIN), F32),
            pltpu.VMEM((NC, SUB, WIN), F32),
            pltpu.VMEM((BATCH * SUB * PAD, WIN), F32),
            pltpu.VMEM((176, len(ALL) * NC * SUB), BF16),
            pltpu.VMEM((624, len(MOST) * NX * SUB), BF16),
            pltpu.VMEM((96, len(ALL) * NX * SUB), BF16),
        ],
        compiler_params=pltpu.CompilerParams(vmem_limit_bytes=24 * 1024 * 1024),
        name="react",
    )(recv, lanes, message, stoich, logk)


def body(cell_state, inflow, courant, pick, node_slot, stoich, logk):
    everywhere = ("z", "y", "h", "q")
    column = lax.axis_index("h") * SIDE + lax.axis_index("q")
    route = []
    for z in range(SIDE):
        for y in range(SIDE):
            for x in range(SIDE):
                for h in range(2):
                    source = (z * SIDE + y) * 2 * SIDE + x * 2 + h
                    route.append((source, (x * SIDE + y) * 2 * SIDE + h * SIDE + z))
    send = cells_to_send(column[None], cell_state, pick)
    recv = lax.all_to_all(send, ("z", "y"), 0, 0, tiled=True)
    slots, message = pack(node_slot, courant, inflow)
    message = lax.ppermute(message, everywhere, route)
    lanes = lax.ppermute(locate(recv, slots), everywhere, route)
    sums = react(recv, lanes, message, stoich, logk)
    back = lax.all_to_all(sums, ("z", "y"), 0, 0, tiled=True)
    return mean(back)


def solution(mesh):
    grid = Mesh(mesh.devices.reshape(SIDE, SIDE, 2, SIDE), ("z", "y", "h", "q"))
    flow, group = ("z", "y"), ("h", "q")
    every = P(None, flow + group)
    placed = (P(None, flow), every, every, P(group, flow, None, None), every, P(), P())
    return jax.shard_map(body, mesh=grid, in_specs=placed, out_specs=every, check_vma=False)
```

```python
import functools

import jax
import jax.numpy as jnp
from jax import lax
from jax.experimental import pallas as pl
from jax.experimental.pallas import tpu as pltpu
from jax.sharding import Mesh, PartitionSpec as P

ITERS = 4
WIN = 128
NC = 12
NX = 6
NQ = NC + NX + 1
PAD = 24
SIDE = 4
FLOW = 16
SUB = 8
HALF = 64
LANES = 2 * WIN + FLOW
BATCH = 8
BF16 = jnp.bfloat16
F32 = jnp.float32


def split(value, parts):
    out = []
    for part in range(parts):
        out.append(value.astype(BF16))
        if part < parts - 1:
            value = value - out[-1].astype(F32)
    return out


def dot(left, right):
    return jnp.dot(left, right, preferred_element_type=F32)


ALL = [(0, 0), (0, 1), (0, 2), (1, 0), (1, 1), (2, 0)]
MOST = ALL[:5]


def stack(parts, terms):
    return jnp.concatenate([parts[right] for _, right in terms], axis=0)


def build_tables(stoich_ref, gram_ref, cross_ref, back_ref):
    def spread(count, terms, pick):
        lane = lax.broadcasted_iota(jnp.int32, (SUB, len(terms) * count * SUB), 1)
        row = lax.broadcasted_iota(jnp.int32, lane.shape, 0)
        which = lane % (count * SUB) // SUB
        vectors = []
        for outer in range(NC + NX - count):
            value = jnp.zeros(lane.shape, F32)
            for inner in range(count):
                value = jnp.where(which == inner, pick(outer, inner), value)
            vectors.append(value)
        return vectors, lane // (count * SUB), lane % SUB == row

    def write(ref, values, term, same, terms):
        for at in range(0, len(values), 2):
            value = jnp.concatenate([jnp.where(same, v, 0.0) for v in values[at : at + 2]], axis=0)
            where = jnp.concatenate([term] * len(values[at : at + 2]), axis=0)
            parts = split(value, 3)
            out = parts[0].astype(F32)
            for k, (left, _) in enumerate(terms):
                if left:
                    out = jnp.where(where == k, parts[left].astype(F32), out)
            ref[pl.ds(SUB * at, out.shape[0]), :] = out.astype(BF16)

    rows, term, same = spread(NC, ALL, lambda p, i: stoich_ref[p, i])
    products = [rows[p] * rows[q] for p, q in pairs(NX)]
    write(gram_ref, products + [jnp.zeros_like(products[0])], term, same, ALL)
    rows, term, same = spread(NX, ALL, lambda i, p: stoich_ref[p, i])
    write(back_ref, rows, term, same, ALL)
    rows, term, same = spread(NX, MOST, lambda i, p: stoich_ref[p, i])
    write(cross_ref, [rows[i] * rows[j] for i, j in pairs(NC)], term, same, MOST)


def tables(stoich):
    return pl.pallas_call(
        build_tables,
        out_shape=(
            jax.ShapeDtypeStruct((176, len(ALL) * NC * SUB), BF16),
            jax.ShapeDtypeStruct((624, len(MOST) * NX * SUB), BF16),
            jax.ShapeDtypeStruct((96, len(ALL) * NX * SUB), BF16),
        ),
        in_specs=[pl.BlockSpec(memory_space=pltpu.SMEM)],
        compiler_params=pltpu.CompilerParams(vmem_limit_bytes=8 * 1024 * 1024),
        name="tables",
    )(stoich)


def cells_kernel(column_ref, cell_ref, pick_ref, out_ref, lanes_ref):
    for y in range(SIDE):
        for kt in range(SUB):
            value = cell_ref[:, pl.ds((y * SUB + kt) * WIN, WIN)]
            for z in range(SIDE):
                out_ref[z * SIDE + y, pl.ds(kt, NC, stride=SUB), :] = value
    for kt in range(SUB):
        lanes = jnp.bitwise_and(pick_ref[0, 0, :, pl.ds(kt * WIN, WIN)], WIN - 1).astype(F32)
        lanes_ref[pl.ds(kt, FLOW, stride=SUB), :] = lanes
    for b in range(FLOW):
        out_ref[b, pl.ds(NC * SUB, SUB), :] = lanes_ref[pl.ds(b * SUB, SUB), :]


def cells_to_send(column, cell_state, pick):
    block = SIDE * SUB * WIN
    return pl.pallas_call(
        cells_kernel,
        out_shape=jax.ShapeDtypeStruct((FLOW, (NC + 1) * SUB, WIN), F32),
        grid_spec=pltpu.PrefetchScalarGridSpec(
            num_scalar_prefetch=1,
            grid=(1,),
            in_specs=[
                pl.BlockSpec((NC, block), lambda step, column: (0, column[0])),
                pl.BlockSpec((1, 1, FLOW, SUB * WIN), lambda step, column: (0, 0, 0, 0)),
            ],
            out_specs=pl.BlockSpec((FLOW, (NC + 1) * SUB, WIN), lambda step, column: (0, 0, 0)),
            scratch_shapes=[pltpu.VMEM((FLOW * SUB, WIN), F32)],
        ),
        name="cells",
    )(column, cell_state, pick)


def locate_kernel(recv_ref, slots_ref, lanes_ref):
    for source in range(FLOW):
        rows = pl.ds(source * SUB, SUB)
        lane = recv_ref[source, pl.ds(NC * SUB, SUB), :]
        lanes_ref[rows, :] = jnp.take_along_axis(lane, slots_ref[rows, :], axis=1)


def locate(recv, slots):
    return pl.pallas_call(
        locate_kernel,
        out_shape=jax.ShapeDtypeStruct(slots.shape, F32),
        in_specs=[pl.BlockSpec(memory_space=pltpu.VMEM)] * 2,
        compiler_params=pltpu.CompilerParams(vmem_limit_bytes=8 * 1024 * 1024),
        name="locate",
    )(recv, slots)


def pack_kernel(slot_ref, courant_ref, inflow_ref, slots_ref, message_ref, first_buf, second_buf):
    def rows(ref, buffer, value):
        buffer[...] = jnp.transpose(value)
        even = buffer[pl.ds(0, WIN, stride=2), :]
        odd = buffer[pl.ds(1, WIN, stride=2), :]
        ref[...] = jnp.concatenate([even, odd], axis=1)

    rows(slots_ref, first_buf, jnp.bitwise_and(slot_ref[...], WIN - 1))
    rows(message_ref.at[pl.ds(0, WIN)], second_buf, courant_ref[...])
    first = inflow_ref[...]
    message_ref[pl.ds(WIN, NC), :] = jnp.concatenate([first, first], axis=1)
    message_ref[pl.ds(WIN + NC, FLOW - NC), :] = jnp.zeros((FLOW - NC, WIN), F32)


def pack(node_slot, courant, inflow):
    return pl.pallas_call(
        pack_kernel,
        out_shape=(
            jax.ShapeDtypeStruct((WIN, WIN), jnp.int32),
            jax.ShapeDtypeStruct((WIN + FLOW, WIN), F32),
        ),
        in_specs=[pl.BlockSpec(memory_space=pltpu.VMEM)] * 3,
        scratch_shapes=[
            pltpu.VMEM((2 * WIN, HALF), jnp.int32),
            pltpu.VMEM((2 * WIN, HALF), F32),
        ],
        compiler_params=pltpu.CompilerParams(vmem_limit_bytes=8 * 1024 * 1024),
        name="pack",
    )(node_slot.T, courant.T, inflow)


def mean_kernel(sums_ref, out_ref):
    for y in range(SIDE):
        for kt in range(SUB):
            total = sums_ref[y, pl.ds(kt, NQ, stride=SUB), :]
            for z in range(1, SIDE):
                total = total + sums_ref[z * SIDE + y, pl.ds(kt, NQ, stride=SUB), :]
            share = 1.0 / jnp.maximum(total[NQ - 1 :, :], 1.0)
            out_ref[:, pl.ds((y * SUB + kt) * WIN, WIN)] = total[: NQ - 1] * share


def mean(sums):
    return pl.pallas_call(
        mean_kernel,
        out_shape=jax.ShapeDtypeStruct((NQ - 1, SIDE * SUB * WIN), F32),
        in_specs=[pl.BlockSpec(memory_space=pltpu.VMEM)],
        compiler_params=pltpu.CompilerParams(vmem_limit_bytes=8 * 1024 * 1024),
        name="mean",
    )(sums)


def pairs(order):
    return [(i, j) for i in range(order) for j in range(i + 1)]


def solve_spd(matrix, rhs):
    order = len(rhs)
    lower, inverse, middle = {}, [], []
    for outer in range(order):
        scaled = {}
        for inner in range(outer):
            total = matrix(outer, inner)
            for other in range(inner):
                total = total - scaled[other] * lower[inner, other]
            scaled[inner] = total
            lower[outer, inner] = total * inverse[inner]
        total = matrix(outer, outer)
        value = rhs[outer]
        for other in range(outer):
            total = total - scaled[other] * lower[outer, other]
            value = value - lower[outer, other] * middle[other]
        inverse.append(1.0 / total)
        middle.append(value)
    result = [None] * order
    for outer in reversed(range(order)):
        total = middle[outer] * inverse[outer]
        for other in range(outer + 1, order):
            total = total - lower[other, outer] * result[other]
        result[outer] = total
    return result


def entries(value, diagonal):
    order = len(diagonal)
    at = {pair: SUB * k for k, pair in enumerate(pairs(order))}

    def entry(i, j):
        part = value[at[i, j] : at[i, j] + SUB]
        return part + diagonal[i] if i == j else part

    return entry


def speciate(totals, stoich, logk, gram, cross, back):
    def log_complexes(logfree):
        out = []
        for p in range(NX):
            total = logk(p)
            for i in range(NC):
                total = total + stoich(p, i) * logfree[i]
            out.append(total)
        return out

    def spread(parts):
        taken = dot(back, stack(parts, ALL))
        return [taken[SUB * i : SUB * (i + 1)] for i in range(NC)]

    logfree = [jnp.log(t) for t in totals]
    invfree = [1.0 / t for t in totals]
    weights = dot(gram, stack(split(jnp.concatenate(invfree, axis=0), 3), ALL))
    logc = log_complexes(logfree)
    inverse = [jnp.exp(-jnp.maximum(v, -80.0)) for v in logc]
    bound = solve_spd(entries(weights, inverse), [jnp.ones_like(totals[0])] * NX)
    taken = spread(split(jnp.concatenate(bound, axis=0), 3))
    logfree = [x - b * v for x, b, v in zip(logfree, taken, invfree)]
    logc = [v + (b * e - 1.0) for v, b, e in zip(logc, bound, inverse)]
    for sweep in range(ITERS - 1):
        free = [jnp.exp(x) for x in logfree]
        if sweep:
            logc = log_complexes(logfree)
        complexes = [jnp.exp(v) for v in logc]
        parts = split(jnp.concatenate(complexes, axis=0), 3)
        jacobian = entries(dot(cross, stack(parts, MOST)), free)
        excess = [(t - f) - b for t, f, b in zip(totals, free, spread(parts))]
        logfree = [x + d for x, d in zip(logfree, solve_spd(jacobian, excess))]
    return [jnp.exp(x) for x in logfree] + [jnp.exp(v) for v in log_complexes(logfree)]


def react_kernel(
    recv_ref, lanes_ref, message_ref, gram_ref, cross_ref, back_ref, stoich_ref, logk_ref,
    out_ref, coef, carry, rows_buf,
):
    lane = lax.broadcasted_iota(jnp.int32, (SUB, WIN), 1)
    row = lax.broadcasted_iota(jnp.int32, (SUB, WIN), 0)
    cell = lax.broadcasted_iota(jnp.int32, (WIN, WIN), 0)
    odd = lane >= HALF
    none = jnp.zeros((WIN, WIN), BF16)
    for p in range(NX):
        for i in range(NC):
            coef[p * NC + i] = jnp.full((SUB, WIN), stoich_ref[p, i], F32)
        coef[NX * NC + p] = jnp.full((SUB, WIN), logk_ref[p], F32)
    rows_buf[...] = jnp.zeros(rows_buf.shape, F32)
    for b in range(BATCH):
        rows_buf[pl.ds(b * SUB * PAD + NQ - 1, SUB, stride=PAD), :] = jnp.ones((SUB, WIN), F32)
    for c in range(NC):
        carry[c] = jnp.broadcast_to(message_ref[pl.ds(WIN + c, 1), :], (SUB, WIN))

    def swap(value):
        return pltpu.roll(value, HALF, 1)

    def wide(value):
        return jnp.concatenate([value] * BATCH, axis=1)

    def step(index, unused):
        moved = [[] for _ in range(NC)]
        places = []
        for b in range(BATCH):
            source = index * BATCH + b
            base = pl.multiple_of(source * SUB, SUB)
            local = lanes_ref[pl.ds(base, SUB), :].astype(jnp.int32)
            places.append(local)
            courant = message_ref[pl.ds(base, SUB), :]
            ratio = 1.0 / (1.0 + courant)
            weight = courant * ratio
            pair = jnp.where(odd, weight * swap(weight), weight)
            run = jnp.where(odd, pair, swap(pair))
            factors = []
            for reach in (1, 2, 4):
                factors.append(jnp.where(row >= reach, run, 0.0))
                run = run * jnp.where(row >= reach, pltpu.roll(run, reach, 0), 1.0)
            for c in range(NC):
                part = jnp.take_along_axis(recv_ref[source, pl.ds(SUB * c, SUB), :], local, axis=1) * ratio
                part = jnp.where(odd, weight * swap(part) + part, part)
                total = jnp.where(odd, part, swap(part))
                for level, reach in enumerate((1, 2, 4)):
                    total = total + factors[level] * pltpu.roll(total, reach, 0)
                before = carry[c]
                total = total + run * before
                carry[c] = jnp.broadcast_to(total[SUB - 1 :, :], (SUB, WIN))
                ahead = jnp.where(row == 0, before, pltpu.roll(total, 1, 0))
                moved[c].append(part + pair * ahead)
        species = speciate(
            [jnp.concatenate(parts, axis=1) for parts in moved],
            lambda p, i: wide(coef[p * NC + i]),
            lambda p: wide(coef[NX * NC + p]),
            gram_ref[:168],
            cross_ref[...],
            back_ref[...],
        )
        for q in range(NC + NX):
            for b in range(BATCH):
                rows_buf[pl.ds(b * SUB * PAD + q, SUB, stride=PAD), :] = species[q][
                    :, b * WIN : (b + 1) * WIN
                ]
        for b in range(BATCH):
            for kt in range(0, SUB, 2):
                hots, values = [], []
                for k in (kt, kt + 1):
                    place = jnp.broadcast_to(places[b][k : k + 1, :], (WIN, WIN))
                    hots.append((cell == place).astype(BF16))
                    value = rows_buf[pl.ds((b * SUB + k) * PAD, PAD), :]
                    values.append(jnp.concatenate(split(value, 2), axis=0))
                upper = jnp.concatenate([hots[0], none], axis=1)
                hot = jnp.concatenate([upper, jnp.concatenate([none, hots[1]], axis=1)], axis=0)
                both = lax.dot_general(
                    jnp.concatenate(values, axis=1),
                    hot,
                    (((1,), (1,)), ((), ())),
                    preferred_element_type=F32,
                )
                sums = both[:PAD] + both[PAD:]
                for k in (0, 1):
                    part = sums[:NQ, k * WIN : (k + 1) * WIN]
                    out_ref[index * BATCH + b, pl.ds(kt + k, NQ, stride=SUB), :] = part
        return unused

    lax.fori_loop(0, FLOW // BATCH, step, 0)


def react(recv, lanes, message, coefficients, stoich, logk):
    return pl.pallas_call(
        react_kernel,
        out_shape=jax.ShapeDtypeStruct((FLOW, NQ * SUB, WIN), F32),
        in_specs=[pl.BlockSpec(memory_space=pltpu.VMEM)] * 6
        + [pl.BlockSpec(memory_space=pltpu.SMEM)] * 2,
        scratch_shapes=[
            pltpu.VMEM((NX * NC + NX, SUB, WIN), F32),
            pltpu.VMEM((NC, SUB, WIN), F32),
            pltpu.VMEM((BATCH * SUB * PAD, WIN), F32),
        ],
        compiler_params=pltpu.CompilerParams(vmem_limit_bytes=24 * 1024 * 1024),
        name="react",
    )(recv, lanes, message, *coefficients, stoich, logk)


def body(cell_state, inflow, courant, pick, node_slot, stoich, logk):
    everywhere = ("z", "y", "h", "q")
    column = lax.axis_index("h") * SIDE + lax.axis_index("q")
    route = []
    for z in range(SIDE):
        for y in range(SIDE):
            for x in range(SIDE):
                for h in range(2):
                    source = (z * SIDE + y) * 2 * SIDE + x * 2 + h
                    away = (x - 2 * h - z // 2) % SIDE
                    to = (z + (2, 1, 0, 3)[away]) % SIDE
                    route.append((source, (to * SIDE + y) * 2 * SIDE + h * SIDE + z))
    send = cells_to_send(column[None], cell_state, pick)
    recv = lax.all_to_all(send, ("z", "y"), 0, 0, tiled=True)
    slots, message = pack(node_slot, courant, inflow)
    message = lax.ppermute(message, everywhere, route)
    lanes = lax.ppermute(locate(recv, slots), everywhere, route)
    sums = react(recv, lanes, message, tables(stoich), stoich, logk)
    back = lax.all_to_all(sums, ("z", "y"), 0, 0, tiled=True)
    return mean(back)


def solution(mesh):
    grid = Mesh(mesh.devices.reshape(SIDE, SIDE, 2, SIDE), ("z", "y", "h", "q"))
    flow, group = ("z", "y"), ("h", "q")
    every = P(None, flow + group)
    placed = (P(None, flow), every, every, P(group, flow, None, None), every, P(), P())
    return jax.shard_map(body, mesh=grid, in_specs=placed, out_specs=every, check_vma=False)
```

```python
import functools

import jax
import jax.numpy as jnp
from jax import lax
from jax.experimental import pallas as pl
from jax.experimental.pallas import tpu as pltpu
from jax.sharding import Mesh, PartitionSpec as P

ITERS = 4
WIN = 128
NC = 12
NX = 6
NQ = NC + NX + 1
PAD = 24
SIDE = 4
FLOW = 16
SUB = 8
HALF = 64
LANES = 2 * WIN + FLOW
BATCH = 8
BF16 = jnp.bfloat16
F32 = jnp.float32


def split(value, parts):
    out = []
    for part in range(parts):
        out.append(value.astype(BF16))
        if part < parts - 1:
            value = value - out[-1].astype(F32)
    return out


def dot(left, right):
    return jnp.dot(left, right, preferred_element_type=F32)


ALL = [(0, 0), (0, 1), (0, 2), (1, 0), (1, 1), (2, 0)]
MOST = ALL[:5]


def stack(parts, terms):
    return jnp.concatenate([parts[right] for _, right in terms], axis=0)


def build_tables(stoich_ref, gram_ref, cross_ref, back_ref):
    def spread(count, terms, pick):
        lane = lax.broadcasted_iota(jnp.int32, (SUB, len(terms) * count * SUB), 1)
        row = lax.broadcasted_iota(jnp.int32, lane.shape, 0)
        which = lane % (count * SUB) // SUB
        vectors = []
        for outer in range(NC + NX - count):
            value = jnp.zeros(lane.shape, F32)
            for inner in range(count):
                value = jnp.where(which == inner, pick(outer, inner), value)
            vectors.append(value)
        return vectors, lane // (count * SUB), lane % SUB == row

    def write(ref, values, term, same, terms):
        for at in range(0, len(values), 2):
            value = jnp.concatenate([jnp.where(same, v, 0.0) for v in values[at : at + 2]], axis=0)
            where = jnp.concatenate([term] * len(values[at : at + 2]), axis=0)
            parts = split(value, 3)
            out = parts[0].astype(F32)
            for k, (left, _) in enumerate(terms):
                if left:
                    out = jnp.where(where == k, parts[left].astype(F32), out)
            ref[pl.ds(SUB * at, out.shape[0]), :] = out.astype(BF16)

    rows, term, same = spread(NC, ALL, lambda p, i: stoich_ref[p, i])
    products = [rows[p] * rows[q] for p, q in pairs(NX)]
    write(gram_ref, products + [jnp.zeros_like(products[0])], term, same, ALL)
    rows, term, same = spread(NX, ALL, lambda i, p: stoich_ref[p, i])
    write(back_ref, rows, term, same, ALL)
    rows, term, same = spread(NX, MOST, lambda i, p: stoich_ref[p, i])
    write(cross_ref, [rows[i] * rows[j] for i, j in pairs(NC)], term, same, MOST)


def tables(stoich):
    return pl.pallas_call(
        build_tables,
        out_shape=(
            jax.ShapeDtypeStruct((176, len(ALL) * NC * SUB), BF16),
            jax.ShapeDtypeStruct((624, len(MOST) * NX * SUB), BF16),
            jax.ShapeDtypeStruct((96, len(ALL) * NX * SUB), BF16),
        ),
        in_specs=[pl.BlockSpec(memory_space=pltpu.SMEM)],
        compiler_params=pltpu.CompilerParams(vmem_limit_bytes=8 * 1024 * 1024),
        name="tables",
    )(stoich)


def cells_kernel(column_ref, cell_ref, pick_ref, out_ref, lanes_ref, part_ref):
    blank = jnp.zeros((FLOW - NC, WIN), F32)
    for y in range(SIDE):
        for kt in range(SUB):
            value = cell_ref[:, pl.ds((y * SUB + kt) * WIN, WIN)]
            value = jnp.concatenate([value, blank], axis=0)
            part_ref[y, pl.ds(kt, FLOW, stride=SUB), :] = value
        for z in range(SIDE):
            rows = pl.ds(0, NC * SUB)
            out_ref[z * SIDE + y, rows, :] = part_ref[y, rows, :]
    for kt in range(SUB):
        lanes = jnp.bitwise_and(pick_ref[0, 0, :, pl.ds(kt * WIN, WIN)], WIN - 1).astype(F32)
        lanes_ref[pl.ds(kt, FLOW, stride=SUB), :] = lanes
    for b in range(FLOW):
        out_ref[b, pl.ds(NC * SUB, SUB), :] = lanes_ref[pl.ds(b * SUB, SUB), :]


def cells_to_send(column, cell_state, pick):
    block = SIDE * SUB * WIN
    return pl.pallas_call(
        cells_kernel,
        out_shape=jax.ShapeDtypeStruct((FLOW, (NC + 1) * SUB, WIN), F32),
        grid_spec=pltpu.PrefetchScalarGridSpec(
            num_scalar_prefetch=1,
            grid=(1,),
            in_specs=[
                pl.BlockSpec((NC, block), lambda step, column: (0, column[0])),
                pl.BlockSpec((1, 1, FLOW, SUB * WIN), lambda step, column: (0, 0, 0, 0)),
            ],
            out_specs=pl.BlockSpec((FLOW, (NC + 1) * SUB, WIN), lambda step, column: (0, 0, 0)),
            scratch_shapes=[
                pltpu.VMEM((FLOW * SUB, WIN), F32),
                pltpu.VMEM((SIDE, FLOW * SUB, WIN), F32),
            ],
        ),
        name="cells",
    )(column, cell_state, pick)


def locate_kernel(recv_ref, slots_ref, lanes_ref):
    for source in range(FLOW):
        rows = pl.ds(source * SUB, SUB)
        lane = recv_ref[source, pl.ds(NC * SUB, SUB), :]
        lanes_ref[rows, :] = jnp.take_along_axis(lane, slots_ref[rows, :], axis=1)


def locate(recv, slots):
    return pl.pallas_call(
        locate_kernel,
        out_shape=jax.ShapeDtypeStruct(slots.shape, F32),
        in_specs=[pl.BlockSpec(memory_space=pltpu.VMEM)] * 2,
        compiler_params=pltpu.CompilerParams(vmem_limit_bytes=8 * 1024 * 1024),
        name="locate",
    )(recv, slots)


def pack_kernel(slot_ref, courant_ref, inflow_ref, slots_ref, message_ref, first_buf, second_buf):
    def rows(ref, buffer, value):
        buffer[...] = jnp.transpose(value)
        even = buffer[pl.ds(0, WIN, stride=2), :]
        odd = buffer[pl.ds(1, WIN, stride=2), :]
        ref[...] = jnp.concatenate([even, odd], axis=1)

    rows(slots_ref, first_buf, jnp.bitwise_and(slot_ref[...], WIN - 1))
    rows(message_ref.at[pl.ds(0, WIN)], second_buf, courant_ref[...])
    first = inflow_ref[...]
    message_ref[pl.ds(WIN, NC), :] = jnp.concatenate([first, first], axis=1)
    message_ref[pl.ds(WIN + NC, FLOW - NC), :] = jnp.zeros((FLOW - NC, WIN), F32)


def pack(node_slot, courant, inflow):
    return pl.pallas_call(
        pack_kernel,
        out_shape=(
            jax.ShapeDtypeStruct((WIN, WIN), jnp.int32),
            jax.ShapeDtypeStruct((WIN + FLOW, WIN), F32),
        ),
        in_specs=[pl.BlockSpec(memory_space=pltpu.VMEM)] * 3,
        scratch_shapes=[
            pltpu.VMEM((2 * WIN, HALF), jnp.int32),
            pltpu.VMEM((2 * WIN, HALF), F32),
        ],
        compiler_params=pltpu.CompilerParams(vmem_limit_bytes=8 * 1024 * 1024),
        name="pack",
    )(node_slot.T, courant.T, inflow)


def mean_kernel(sums_ref, out_ref, rows_buf):
    for y in range(SIDE):
        totals = []
        for q in range(NQ):
            rows = pl.ds(q * SUB, SUB)
            total = sums_ref[y, rows, :]
            for z in range(1, SIDE):
                total = total + sums_ref[z * SIDE + y, rows, :]
            totals.append(total)
        share = 1.0 / jnp.maximum(totals[NQ - 1], 1.0)
        for q in range(NQ - 1):
            rows_buf[y, pl.ds(q, SUB, stride=PAD), :] = totals[q] * share
        for kt in range(SUB):
            part = rows_buf[y, pl.ds(kt * PAD, PAD), :]
            out_ref[:, pl.ds((y * SUB + kt) * WIN, WIN)] = part[: NQ - 1]


def mean(sums):
    return pl.pallas_call(
        mean_kernel,
        out_shape=jax.ShapeDtypeStruct((NQ - 1, SIDE * SUB * WIN), F32),
        in_specs=[pl.BlockSpec(memory_space=pltpu.VMEM)],
        scratch_shapes=[pltpu.VMEM((SIDE, SUB * PAD, WIN), F32)],
        compiler_params=pltpu.CompilerParams(vmem_limit_bytes=8 * 1024 * 1024),
        name="mean",
    )(sums)


def pairs(order):
    return [(i, j) for i in range(order) for j in range(i + 1)]


def solve_spd(matrix, rhs):
    order = len(rhs)
    lower, inverse, middle = {}, [], []
    for outer in range(order):
        scaled = {}
        for inner in range(outer):
            total = matrix(outer, inner)
            for other in range(inner):
                total = total - scaled[other] * lower[inner, other]
            scaled[inner] = total
            lower[outer, inner] = total * inverse[inner]
        total = matrix(outer, outer)
        value = rhs[outer]
        for other in range(outer):
            total = total - scaled[other] * lower[outer, other]
            value = value - lower[outer, other] * middle[other]
        inverse.append(1.0 / total)
        middle.append(value)
    result = [None] * order
    for outer in reversed(range(order)):
        total = middle[outer] * inverse[outer]
        for other in range(outer + 1, order):
            total = total - lower[other, outer] * result[other]
        result[outer] = total
    return result


def entries(value, diagonal):
    order = len(diagonal)
    at = {pair: SUB * k for k, pair in enumerate(pairs(order))}

    def entry(i, j):
        part = value[at[i, j] : at[i, j] + SUB]
        return part + diagonal[i] if i == j else part

    return entry


def speciate(totals, stoich, logk, gram, cross, back):
    def log_complexes(logfree):
        out = []
        for p in range(NX):
            total = logk(p)
            for i in range(NC):
                total = total + stoich(p, i) * logfree[i]
            out.append(total)
        return out

    def spread(parts):
        taken = dot(back, stack(parts, ALL))
        return [taken[SUB * i : SUB * (i + 1)] for i in range(NC)]

    logfree = [jnp.log(t) for t in totals]
    invfree = [1.0 / t for t in totals]
    weights = dot(gram, stack(split(jnp.concatenate(invfree, axis=0), 3), ALL))
    logc = log_complexes(logfree)
    inverse = [jnp.exp(-jnp.maximum(v, -80.0)) for v in logc]
    bound = solve_spd(entries(weights, inverse), [jnp.ones_like(totals[0])] * NX)
    taken = spread(split(jnp.concatenate(bound, axis=0), 3))
    logfree = [x - b * v for x, b, v in zip(logfree, taken, invfree)]
    logc = [v + (b * e - 1.0) for v, b, e in zip(logc, bound, inverse)]
    for sweep in range(ITERS - 1):
        free = [jnp.exp(x) for x in logfree]
        if sweep:
            logc = log_complexes(logfree)
        complexes = [jnp.exp(v) for v in logc]
        parts = split(jnp.concatenate(complexes, axis=0), 3)
        jacobian = entries(dot(cross, stack(parts, MOST)), free)
        excess = [(t - f) - b for t, f, b in zip(totals, free, spread(parts))]
        logfree = [x + d for x, d in zip(logfree, solve_spd(jacobian, excess))]
    return [jnp.exp(x) for x in logfree] + [jnp.exp(v) for v in log_complexes(logfree)]


def react_kernel(
    recv_ref, lanes_ref, message_ref, gram_ref, cross_ref, back_ref, stoich_ref, logk_ref,
    out_ref, coef, carry, rows_buf, sums_buf,
):
    lane = lax.broadcasted_iota(jnp.int32, (SUB, WIN), 1)
    row = lax.broadcasted_iota(jnp.int32, (SUB, WIN), 0)
    cell = lax.broadcasted_iota(jnp.int32, (WIN, WIN), 0)
    odd = lane >= HALF
    none = jnp.zeros((WIN, WIN), BF16)
    for p in range(NX):
        for i in range(NC):
            coef[p * NC + i] = jnp.full((SUB, WIN), stoich_ref[p, i], F32)
        coef[NX * NC + p] = jnp.full((SUB, WIN), logk_ref[p], F32)
    rows_buf[...] = jnp.zeros(rows_buf.shape, F32)
    for b in range(BATCH):
        rows_buf[pl.ds(b * SUB * PAD + NQ - 1, SUB, stride=PAD), :] = jnp.ones((SUB, WIN), F32)
    for c in range(NC):
        carry[c] = jnp.broadcast_to(message_ref[pl.ds(WIN + c, 1), :], (SUB, WIN))

    def swap(value):
        return pltpu.roll(value, HALF, 1)

    def wide(value):
        return jnp.concatenate([value] * BATCH, axis=1)

    def step(index, unused):
        moved = [[] for _ in range(NC)]
        places = []
        for b in range(BATCH):
            source = index * BATCH + b
            base = pl.multiple_of(source * SUB, SUB)
            local = lanes_ref[pl.ds(base, SUB), :].astype(jnp.int32)
            places.append(local)
            courant = message_ref[pl.ds(base, SUB), :]
            ratio = 1.0 / (1.0 + courant)
            weight = courant * ratio
            pair = jnp.where(odd, weight * swap(weight), weight)
            run = jnp.where(odd, pair, swap(pair))
            factors = []
            for reach in (1, 2, 4):
                factors.append(jnp.where(row >= reach, run, 0.0))
                run = run * jnp.where(row >= reach, pltpu.roll(run, reach, 0), 1.0)
            for c in range(NC):
                part = jnp.take_along_axis(recv_ref[source, pl.ds(SUB * c, SUB), :], local, axis=1) * ratio
                part = jnp.where(odd, weight * swap(part) + part, part)
                total = jnp.where(odd, part, swap(part))
                for level, reach in enumerate((1, 2, 4)):
                    total = total + factors[level] * pltpu.roll(total, reach, 0)
                before = carry[c]
                total = total + run * before
                carry[c] = jnp.broadcast_to(total[SUB - 1 :, :], (SUB, WIN))
                ahead = jnp.where(row == 0, before, pltpu.roll(total, 1, 0))
                moved[c].append(part + pair * ahead)
        species = speciate(
            [jnp.concatenate(parts, axis=1) for parts in moved],
            lambda p, i: wide(coef[p * NC + i]),
            lambda p: wide(coef[NX * NC + p]),
            gram_ref[...],
            cross_ref[...],
            back_ref[...],
        )
        for q in range(NC + NX):
            for b in range(BATCH):
                rows_buf[pl.ds(b * SUB * PAD + q, SUB, stride=PAD), :] = species[q][
                    :, b * WIN : (b + 1) * WIN
                ]
        for b in range(BATCH):
            for kt in range(0, SUB, 2):
                hots, values = [], []
                for k in (kt, kt + 1):
                    place = jnp.broadcast_to(places[b][k : k + 1, :], (WIN, WIN))
                    hots.append((cell == place).astype(BF16))
                    value = rows_buf[pl.ds((b * SUB + k) * PAD, PAD), :]
                    values.append(jnp.concatenate(split(value, 2), axis=0))
                upper = jnp.concatenate([hots[0], none], axis=1)
                hot = jnp.concatenate([upper, jnp.concatenate([none, hots[1]], axis=1)], axis=0)
                both = lax.dot_general(
                    jnp.concatenate(values, axis=1),
                    hot,
                    (((1,), (1,)), ((), ())),
                    preferred_element_type=F32,
                )
                sums = both[:PAD] + both[PAD:]
                for k in (0, 1):
                    part = sums[:, k * WIN : (k + 1) * WIN]
                    sums_buf[b, pl.ds(kt + k, PAD, stride=SUB), :] = part
            out_ref[index * BATCH + b] = sums_buf[b, pl.ds(0, NQ * SUB), :]
        return unused

    lax.fori_loop(0, FLOW // BATCH, step, 0)


def react(recv, lanes, message, coefficients, stoich, logk):
    return pl.pallas_call(
        react_kernel,
        out_shape=jax.ShapeDtypeStruct((FLOW, NQ * SUB, WIN), F32),
        in_specs=[pl.BlockSpec(memory_space=pltpu.VMEM)] * 6
        + [pl.BlockSpec(memory_space=pltpu.SMEM)] * 2,
        scratch_shapes=[
            pltpu.VMEM((NX * NC + NX, SUB, WIN), F32),
            pltpu.VMEM((NC, SUB, WIN), F32),
            pltpu.VMEM((BATCH * SUB * PAD, WIN), F32),
            pltpu.VMEM((BATCH, SUB * PAD, WIN), F32),
        ],
        compiler_params=pltpu.CompilerParams(vmem_limit_bytes=24 * 1024 * 1024),
        name="react",
    )(recv, lanes, message, *coefficients, stoich, logk)


def body(cell_state, inflow, courant, pick, node_slot, stoich, logk):
    everywhere = ("z", "y", "h", "q")
    column = lax.axis_index("h") * SIDE + lax.axis_index("q")
    route = []
    for z in range(SIDE):
        for y in range(SIDE):
            for x in range(SIDE):
                for h in range(2):
                    source = (z * SIDE + y) * 2 * SIDE + x * 2 + h
                    away = (x - 2 * h - z // 2) % SIDE
                    to = (z + (2, 1, 0, 3)[away]) % SIDE
                    route.append((source, (to * SIDE + y) * 2 * SIDE + h * SIDE + z))
    send = cells_to_send(column[None], cell_state, pick)
    recv = lax.all_to_all(send, ("z", "y"), 0, 0, tiled=True)
    slots, message = pack(node_slot, courant, inflow)
    message = lax.ppermute(message, everywhere, route)
    lanes = lax.ppermute(locate(recv, slots), everywhere, route)
    sums = react(recv, lanes, message, tables(stoich), stoich, logk)
    back = lax.all_to_all(sums, ("z", "y"), 0, 0, tiled=True)
    return mean(back)


def solution(mesh):
    grid = Mesh(mesh.devices.reshape(SIDE, SIDE, 2, SIDE), ("z", "y", "h", "q"))
    flow, group = ("z", "y"), ("h", "q")
    every = P(None, flow + group)
    placed = (P(None, flow), every, every, P(group, flow, None, None), every, P(), P())
    return jax.shard_map(body, mesh=grid, in_specs=placed, out_specs=every, check_vma=False)
```

```python
import functools

import jax
import jax.numpy as jnp
from jax import lax
from jax.experimental import pallas as pl
from jax.experimental.pallas import tpu as pltpu
from jax.sharding import Mesh, PartitionSpec as P

ITERS = 4
WIN = 128
NC = 12
NX = 6
NQ = NC + NX + 1
PAD = 24
SIDE = 4
FLOW = 16
SUB = 8
HALF = 64
LANES = 2 * WIN + FLOW
BATCH = 8
BF16 = jnp.bfloat16
F32 = jnp.float32


def split(value, parts):
    out = []
    for part in range(parts):
        out.append(value.astype(BF16))
        if part < parts - 1:
            value = value - out[-1].astype(F32)
    return out


def dot(left, right):
    return jnp.dot(left, right, preferred_element_type=F32)


ALL = [(0, 0), (0, 1), (0, 2), (1, 0), (1, 1), (2, 0)]
MOST = ALL[:5]


def stack(parts, terms):
    return jnp.concatenate([parts[right] for _, right in terms], axis=0)


def build_tables(stoich_ref, gram_ref, cross_ref, back_ref):
    def spread(count, terms, pick):
        lane = lax.broadcasted_iota(jnp.int32, (SUB, len(terms) * count * SUB), 1)
        row = lax.broadcasted_iota(jnp.int32, lane.shape, 0)
        which = lane % (count * SUB) // SUB
        vectors = []
        for outer in range(NC + NX - count):
            value = jnp.zeros(lane.shape, F32)
            for inner in range(count):
                value = jnp.where(which == inner, pick(outer, inner), value)
            vectors.append(value)
        return vectors, lane // (count * SUB), lane % SUB == row

    def write(ref, values, term, same, terms):
        for at in range(0, len(values), 2):
            value = jnp.concatenate([jnp.where(same, v, 0.0) for v in values[at : at + 2]], axis=0)
            where = jnp.concatenate([term] * len(values[at : at + 2]), axis=0)
            parts = split(value, 3)
            out = parts[0].astype(F32)
            for k, (left, _) in enumerate(terms):
                if left:
                    out = jnp.where(where == k, parts[left].astype(F32), out)
            ref[pl.ds(SUB * at, out.shape[0]), :] = out.astype(BF16)

    rows, term, same = spread(NC, ALL, lambda p, i: stoich_ref[p, i])
    products = [rows[p] * rows[q] for p, q in pairs(NX)]
    write(gram_ref, products + [jnp.zeros_like(products[0])], term, same, ALL)
    rows, term, same = spread(NX, ALL, lambda i, p: stoich_ref[p, i])
    write(back_ref, rows, term, same, ALL)
    rows, term, same = spread(NX, MOST, lambda i, p: stoich_ref[p, i])
    write(cross_ref, [rows[i] * rows[j] for i, j in pairs(NC)], term, same, MOST)


def tables(stoich):
    return pl.pallas_call(
        build_tables,
        out_shape=(
            jax.ShapeDtypeStruct((176, len(ALL) * NC * SUB), BF16),
            jax.ShapeDtypeStruct((624, len(MOST) * NX * SUB), BF16),
            jax.ShapeDtypeStruct((96, len(ALL) * NX * SUB), BF16),
        ),
        in_specs=[pl.BlockSpec(memory_space=pltpu.SMEM)],
        compiler_params=pltpu.CompilerParams(vmem_limit_bytes=8 * 1024 * 1024),
        name="tables",
    )(stoich)


def cells_kernel(column_ref, cell_ref, pick_ref, out_ref, lanes_ref, part_ref):
    blank = jnp.zeros((FLOW - NC, WIN), F32)
    for y in range(SIDE):
        for kt in range(SUB):
            value = cell_ref[:, pl.ds((y * SUB + kt) * WIN, WIN)]
            value = jnp.concatenate([value, blank], axis=0)
            part_ref[y, pl.ds(kt, FLOW, stride=SUB), :] = value
        for z in range(SIDE):
            rows = pl.ds(0, NC * SUB)
            out_ref[z * SIDE + y, rows, :] = part_ref[y, rows, :]
    for kt in range(SUB):
        lanes = jnp.bitwise_and(pick_ref[0, 0, :, pl.ds(kt * WIN, WIN)], WIN - 1).astype(F32)
        lanes_ref[pl.ds(kt, FLOW, stride=SUB), :] = lanes
    for b in range(FLOW):
        out_ref[b, pl.ds(NC * SUB, SUB), :] = lanes_ref[pl.ds(b * SUB, SUB), :]


def cells_to_send(column, cell_state, pick):
    block = SIDE * SUB * WIN
    return pl.pallas_call(
        cells_kernel,
        out_shape=jax.ShapeDtypeStruct((FLOW, (NC + 1) * SUB, WIN), F32),
        grid_spec=pltpu.PrefetchScalarGridSpec(
            num_scalar_prefetch=1,
            grid=(1,),
            in_specs=[
                pl.BlockSpec((NC, block), lambda step, column: (0, column[0])),
                pl.BlockSpec((1, 1, FLOW, SUB * WIN), lambda step, column: (0, 0, 0, 0)),
            ],
            out_specs=pl.BlockSpec(memory_space=pltpu.VMEM),
            scratch_shapes=[
                pltpu.VMEM((FLOW * SUB, WIN), F32),
                pltpu.VMEM((SIDE, FLOW * SUB, WIN), F32),
            ],
        ),
        compiler_params=pltpu.CompilerParams(vmem_limit_bytes=125 * 512 * 1024),
        name="cells",
    )(column, cell_state, pick)


def locate_kernel(recv_ref, slots_ref, lanes_ref):
    for source in range(FLOW):
        rows = pl.ds(source * SUB, SUB)
        lane = recv_ref[source, pl.ds(NC * SUB, SUB), :]
        lanes_ref[rows, :] = jnp.take_along_axis(lane, slots_ref[rows, :], axis=1)


def locate(recv, slots):
    return pl.pallas_call(
        locate_kernel,
        out_shape=jax.ShapeDtypeStruct(slots.shape, F32),
        in_specs=[pl.BlockSpec(memory_space=pltpu.VMEM)] * 2,
        compiler_params=pltpu.CompilerParams(vmem_limit_bytes=8 * 1024 * 1024),
        name="locate",
    )(recv, slots)


def pack_kernel(slot_ref, courant_ref, inflow_ref, slots_ref, message_ref, first_buf, second_buf):
    def rows(ref, buffer, value):
        buffer[...] = jnp.transpose(value)
        even = buffer[pl.ds(0, WIN, stride=2), :]
        odd = buffer[pl.ds(1, WIN, stride=2), :]
        ref[...] = jnp.concatenate([even, odd], axis=1)

    rows(slots_ref, first_buf, jnp.bitwise_and(slot_ref[...], WIN - 1))
    rows(message_ref.at[pl.ds(0, WIN)], second_buf, courant_ref[...])
    first = inflow_ref[...]
    message_ref[pl.ds(WIN, NC), :] = jnp.concatenate([first, first], axis=1)
    message_ref[pl.ds(WIN + NC, FLOW - NC), :] = jnp.zeros((FLOW - NC, WIN), F32)


def pack(node_slot, courant, inflow):
    return pl.pallas_call(
        pack_kernel,
        out_shape=(
            jax.ShapeDtypeStruct((WIN, WIN), jnp.int32),
            jax.ShapeDtypeStruct((WIN + FLOW, WIN), F32),
        ),
        in_specs=[pl.BlockSpec(memory_space=pltpu.VMEM)] * 3,
        scratch_shapes=[
            pltpu.VMEM((2 * WIN, HALF), jnp.int32),
            pltpu.VMEM((2 * WIN, HALF), F32),
        ],
        compiler_params=pltpu.CompilerParams(vmem_limit_bytes=8 * 1024 * 1024),
        name="pack",
    )(node_slot.T, courant.T, inflow)


def mean_kernel(sums_ref, out_ref, rows_buf):
    for y in range(SIDE):
        totals = []
        for q in range(NQ):
            rows = pl.ds(q * SUB, SUB)
            total = sums_ref[y, rows, :]
            for z in range(1, SIDE):
                total = total + sums_ref[z * SIDE + y, rows, :]
            totals.append(total)
        share = 1.0 / jnp.maximum(totals[NQ - 1], 1.0)
        for q in range(NQ - 1):
            rows_buf[y, pl.ds(q, SUB, stride=PAD), :] = totals[q] * share
        for kt in range(SUB):
            part = rows_buf[y, pl.ds(kt * PAD, PAD), :]
            out_ref[:, pl.ds((y * SUB + kt) * WIN, WIN)] = part[: NQ - 1]


def mean(sums):
    return pl.pallas_call(
        mean_kernel,
        out_shape=jax.ShapeDtypeStruct((NQ - 1, SIDE * SUB * WIN), F32),
        in_specs=[pl.BlockSpec(memory_space=pltpu.VMEM)],
        scratch_shapes=[pltpu.VMEM((SIDE, SUB * PAD, WIN), F32)],
        compiler_params=pltpu.CompilerParams(vmem_limit_bytes=8 * 1024 * 1024),
        name="mean",
    )(sums)


def pairs(order):
    return [(i, j) for i in range(order) for j in range(i + 1)]


def solve_spd(matrix, rhs):
    order = len(rhs)
    lower, inverse, middle = {}, [], []
    for outer in range(order):
        scaled = {}
        for inner in range(outer):
            total = matrix(outer, inner)
            for other in range(inner):
                total = total - scaled[other] * lower[inner, other]
            scaled[inner] = total
            lower[outer, inner] = total * inverse[inner]
        total = matrix(outer, outer)
        value = rhs[outer]
        for other in range(outer):
            total = total - scaled[other] * lower[outer, other]
            value = value - lower[outer, other] * middle[other]
        inverse.append(1.0 / total)
        middle.append(value)
    result = [None] * order
    for outer in reversed(range(order)):
        total = middle[outer] * inverse[outer]
        for other in range(outer + 1, order):
            total = total - lower[other, outer] * result[other]
        result[outer] = total
    return result


def entries(value, diagonal):
    order = len(diagonal)
    at = {pair: SUB * k for k, pair in enumerate(pairs(order))}

    def entry(i, j):
        part = value[at[i, j] : at[i, j] + SUB]
        return part + diagonal[i] if i == j else part

    return entry


def speciate(totals, stoich, logk, gram, cross, back):
    def log_complexes(logfree):
        out = []
        for p in range(NX):
            total = logk(p)
            for i in range(NC):
                total = total + stoich(p, i) * logfree[i]
            out.append(total)
        return out

    def spread(parts):
        taken = dot(back, stack(parts, ALL))
        return [taken[SUB * i : SUB * (i + 1)] for i in range(NC)]

    logfree = [jnp.log(t) for t in totals]
    invfree = [1.0 / t for t in totals]
    weights = dot(gram, stack(split(jnp.concatenate(invfree, axis=0), 3), ALL))
    logc = log_complexes(logfree)
    inverse = [jnp.exp(-jnp.maximum(v, -80.0)) for v in logc]
    bound = solve_spd(entries(weights, inverse), [jnp.ones_like(totals[0])] * NX)
    taken = spread(split(jnp.concatenate(bound, axis=0), 3))
    logfree = [x - b * v for x, b, v in zip(logfree, taken, invfree)]
    logc = [v + (b * e - 1.0) for v, b, e in zip(logc, bound, inverse)]
    for sweep in range(ITERS - 1):
        free = [jnp.exp(x) for x in logfree]
        if sweep:
            logc = log_complexes(logfree)
        complexes = [jnp.exp(v) for v in logc]
        parts = split(jnp.concatenate(complexes, axis=0), 3)
        jacobian = entries(dot(cross, stack(parts, MOST)), free)
        excess = [(t - f) - b for t, f, b in zip(totals, free, spread(parts))]
        logfree = [x + d for x, d in zip(logfree, solve_spd(jacobian, excess))]
    return [jnp.exp(x) for x in logfree] + [jnp.exp(v) for v in log_complexes(logfree)]


def react_kernel(
    recv_ref, lanes_ref, message_ref, gram_ref, cross_ref, back_ref, stoich_ref, logk_ref,
    out_ref, coef, carry, rows_buf, sums_buf,
):
    lane = lax.broadcasted_iota(jnp.int32, (SUB, WIN), 1)
    row = lax.broadcasted_iota(jnp.int32, (SUB, WIN), 0)
    cell = lax.broadcasted_iota(jnp.int32, (WIN, WIN), 0)
    odd = lane >= HALF
    none = jnp.zeros((WIN, WIN), BF16)
    for p in range(NX):
        for i in range(NC):
            coef[p * NC + i] = jnp.full((SUB, WIN), stoich_ref[p, i], F32)
        coef[NX * NC + p] = jnp.full((SUB, WIN), logk_ref[p], F32)
    rows_buf[...] = jnp.zeros(rows_buf.shape, F32)
    for b in range(BATCH):
        rows_buf[pl.ds(b * SUB * PAD + NQ - 1, SUB, stride=PAD), :] = jnp.ones((SUB, WIN), F32)
    for c in range(NC):
        carry[c] = jnp.broadcast_to(message_ref[pl.ds(WIN + c, 1), :], (SUB, WIN))

    def swap(value):
        return pltpu.roll(value, HALF, 1)

    def wide(value):
        return jnp.concatenate([value] * BATCH, axis=1)

    def step(index, unused):
        moved = [[] for _ in range(NC)]
        places = []
        for b in range(BATCH):
            source = index * BATCH + b
            base = pl.multiple_of(source * SUB, SUB)
            local = lanes_ref[pl.ds(base, SUB), :].astype(jnp.int32)
            places.append(local)
            courant = message_ref[pl.ds(base, SUB), :]
            ratio = 1.0 / (1.0 + courant)
            weight = courant * ratio
            pair = jnp.where(odd, weight * swap(weight), weight)
            run = jnp.where(odd, pair, swap(pair))
            factors = []
            for reach in (1, 2, 4):
                factors.append(jnp.where(row >= reach, run, 0.0))
                run = run * jnp.where(row >= reach, pltpu.roll(run, reach, 0), 1.0)
            for c in range(NC):
                part = jnp.take_along_axis(recv_ref[source, pl.ds(SUB * c, SUB), :], local, axis=1) * ratio
                part = jnp.where(odd, weight * swap(part) + part, part)
                total = jnp.where(odd, part, swap(part))
                for level, reach in enumerate((1, 2, 4)):
                    total = total + factors[level] * pltpu.roll(total, reach, 0)
                before = carry[c]
                total = total + run * before
                carry[c] = jnp.broadcast_to(total[SUB - 1 :, :], (SUB, WIN))
                ahead = jnp.where(row == 0, before, pltpu.roll(total, 1, 0))
                moved[c].append(part + pair * ahead)
        species = speciate(
            [jnp.concatenate(parts, axis=1) for parts in moved],
            lambda p, i: wide(coef[p * NC + i]),
            lambda p: wide(coef[NX * NC + p]),
            gram_ref[...],
            cross_ref[...],
            back_ref[...],
        )
        for q in range(NC + NX):
            for b in range(BATCH):
                rows_buf[pl.ds(b * SUB * PAD + q, SUB, stride=PAD), :] = species[q][
                    :, b * WIN : (b + 1) * WIN
                ]
        for b in range(BATCH):
            for kt in range(0, SUB, 2):
                hots, values = [], []
                for k in (kt, kt + 1):
                    place = jnp.broadcast_to(places[b][k : k + 1, :], (WIN, WIN))
                    hots.append((cell == place).astype(BF16))
                    value = rows_buf[pl.ds((b * SUB + k) * PAD, PAD), :]
                    values.append(jnp.concatenate(split(value, 2), axis=0))
                upper = jnp.concatenate([hots[0], none], axis=1)
                hot = jnp.concatenate([upper, jnp.concatenate([none, hots[1]], axis=1)], axis=0)
                both = lax.dot_general(
                    jnp.concatenate(values, axis=1),
                    hot,
                    (((1,), (1,)), ((), ())),
                    preferred_element_type=F32,
                )
                sums = both[:PAD] + both[PAD:]
                for k in (0, 1):
                    part = sums[:, k * WIN : (k + 1) * WIN]
                    sums_buf[b, pl.ds(kt + k, PAD, stride=SUB), :] = part
            out_ref[index * BATCH + b] = sums_buf[b, pl.ds(0, NQ * SUB), :]
        return unused

    lax.fori_loop(0, FLOW // BATCH, step, 0)


def react(recv, lanes, message, coefficients, stoich, logk):
    return pl.pallas_call(
        react_kernel,
        out_shape=jax.ShapeDtypeStruct((FLOW, NQ * SUB, WIN), F32),
        in_specs=[pl.BlockSpec(memory_space=pltpu.VMEM)] * 6
        + [pl.BlockSpec(memory_space=pltpu.SMEM)] * 2,
        scratch_shapes=[
            pltpu.VMEM((NX * NC + NX, SUB, WIN), F32),
            pltpu.VMEM((NC, SUB, WIN), F32),
            pltpu.VMEM((BATCH * SUB * PAD, WIN), F32),
            pltpu.VMEM((BATCH, SUB * PAD, WIN), F32),
        ],
        compiler_params=pltpu.CompilerParams(vmem_limit_bytes=24 * 1024 * 1024),
        name="react",
    )(recv, lanes, message, *coefficients, stoich, logk)


def body(cell_state, inflow, courant, pick, node_slot, stoich, logk):
    everywhere = ("z", "y", "h", "q")
    column = lax.axis_index("h") * SIDE + lax.axis_index("q")
    route = []
    for z in range(SIDE):
        for y in range(SIDE):
            for x in range(SIDE):
                for h in range(2):
                    source = (z * SIDE + y) * 2 * SIDE + x * 2 + h
                    away = (x - 2 * h - z // 2) % SIDE
                    to = (z + (2, 1, 0, 3)[away]) % SIDE
                    route.append((source, (to * SIDE + y) * 2 * SIDE + h * SIDE + z))
    send = cells_to_send(column[None], cell_state, pick)
    recv = lax.all_to_all(send, ("z", "y"), 0, 0, tiled=True)
    slots, message = pack(node_slot, courant, inflow)
    message = lax.ppermute(message, everywhere, route)
    lanes = lax.ppermute(locate(recv, slots), everywhere, route)
    sums = react(recv, lanes, message, tables(stoich), stoich, logk)
    back = lax.all_to_all(sums, ("z", "y"), 0, 0, tiled=True)
    return mean(back)


def solution(mesh):
    grid = Mesh(mesh.devices.reshape(SIDE, SIDE, 2, SIDE), ("z", "y", "h", "q"))
    flow, group = ("z", "y"), ("h", "q")
    every = P(None, flow + group)
    placed = (P(None, flow), every, every, P(group, flow, None, None), every, P(), P())
    return jax.shard_map(body, mesh=grid, in_specs=placed, out_specs=every, check_vma=False)
```
